256 devices in a mesh: doc: 16 (over y, x), cent: 16 (over z, core).
Axes of the slice: x: 4, y: 4, z: 8, core: 2. Of those that a mesh axis runs over, the one named last changes fastest.
Arguments:
- documents: bfloat16 [32768, 768], P('doc'), may hold values from -6 to 6
- centroids: bfloat16 [512, 128, 768], P('cent'), may hold values from -6 to 6
- candidates: int32 [256, 128], P('doc', 'cent'), may hold values from 0 to 31, as said below
- counts: int32 [256, 16], P('doc', 'cent'), may hold values from 1 to 8, as said below
Outputs:
- new_centroids: bfloat16 [512, 128, 768], P('cent', 'doc')
The draws below stay inside these ranges and needn't reach their ends.
Inputs may be any that keep to these rules, and one draw needn't show every extreme that they name: `candidates`: within one block's list for one index of cent the 8 group numbers are distinct; entries past the live count name some group and are ignored. `counts`: a live count is reached by some block for some index of cent in every draw at its largest value.
All inputs are finite; a program needn't handle non-finite values.
Results may differ from the reference program's by a relative error of at most 0.013.
Values may be sent and summed in bfloat16 or wider, within the bound.
A program may use at most 192 MiB of HBM per device.

```python
import math
import jax
import jax.numpy as jnp
from jax import lax

E = 768
GROUP = 128
GROUPS_DEV = 32
BLOCK = 128
SLOTS = 8
PASSES = 3
ROWS_DEV = 2048
DOCS = 32768
NBLK = 256
SHARDS = 16
GROUPS = 512
CENTROIDS = 65536
N_DOC = 16


def centroid_base(key):
    key = jax.random.fold_in(key, 41)
    return jnp.clip(jax.random.normal(key, (GROUPS, GROUP, E), jnp.float32), -6.0, 6.0)


def list_draw(key):
    key = jax.random.fold_in(key, 11)
    noise = jax.random.randint(key, (NBLK * SHARDS, GROUPS_DEV), 0, 1 << 20)
    scores = noise * GROUPS_DEV + jnp.arange(GROUPS_DEV, dtype=jnp.int32)[None, :]
    order = jnp.argsort(scores, axis=1)
    picked = order[:, :SLOTS].astype(jnp.int32)
    return picked.reshape(NBLK, SHARDS * SLOTS)


def count_draw(key):
    key = jax.random.fold_in(key, 23)
    key_heavy, key_forced, key_low, key_high, key_row = jax.random.split(key, 5)
    heavy = jax.random.randint(key_heavy, (SHARDS,), 0, 4) == 0
    forced = jax.random.randint(key_forced, (), 0, SHARDS)
    heavy = heavy | (jnp.arange(SHARDS, dtype=jnp.int32) == forced)
    low_counts = jax.random.randint(key_low, (NBLK, SHARDS), 1, SLOTS // 4 + 2)
    high_counts = jax.random.randint(key_high, (NBLK, SHARDS), SLOTS - SLOTS // 4, SLOTS + 1)
    drawn = jnp.where(heavy[None, :], high_counts, low_counts)
    chosen_row = jax.random.randint(key_row, (), 0, NBLK)
    drawn = drawn.at[chosen_row, forced].set(SLOTS)
    return drawn.astype(jnp.int32)


def draw_candidates(key, part):
    return list_draw(key)


def draw_counts(key, part):
    return count_draw(key)


def draw_centroids(key, part):
    base = centroid_base(key)
    values = base
    return values.astype(jnp.bfloat16)


def home_rows(base, listed, live, key):
    key_shard, key_slot, key_member, key_narrow = jax.random.split(key, 4)
    block_of = jnp.arange(DOCS, dtype=jnp.int32) // BLOCK
    shard = jax.random.randint(key_shard, (DOCS,), 0, SHARDS)
    live_here = live[block_of, shard]
    slot = jax.random.randint(key_slot, (DOCS,), 0, 1 << 20) % live_here
    local = listed[block_of, shard * SLOTS + slot]
    group = shard * GROUPS_DEV + local
    wide = jax.random.randint(key_member, (DOCS,), 0, GROUP)
    narrow = jax.random.randint(key_narrow, (DOCS,), 0, 2)
    member = jnp.where(narrow == 1, wide % (GROUP // 4), wide)
    return base[group, member]


def draw_documents(key, part):
    base = centroid_base(key)
    listed = list_draw(key)
    live = count_draw(key)
    key = jax.random.fold_in(key, 31)
    key_first, key_second, key_w1, key_w2, key_noise = jax.random.split(key, 5)
    first = home_rows(base, listed, live, key_first)
    second = home_rows(base, listed, live, key_second)
    weight_one = jax.random.uniform(key_w1, (DOCS, 1), jnp.float32, 0.4, 1.0)
    weight_two = jax.random.uniform(key_w2, (DOCS, 1), jnp.float32, 0.3, 0.9)
    noise = jax.random.normal(key_noise, (DOCS, E), jnp.float32)
    values = weight_one * first + weight_two * second + noise
    return jnp.clip(values, -6.0, 6.0).astype(jnp.bfloat16)


def setup_inputs(seed: int = 0) -> dict:
    splits = jax.random.split(jax.random.key(seed), 5)
    documents = draw_documents(jax.random.fold_in(splits[4], 71), 0)
    centroids = draw_centroids(jax.random.fold_in(splits[4], 71), 0)
    candidates = draw_candidates(jax.random.fold_in(splits[4], 71), 0)
    counts = draw_counts(jax.random.fold_in(splits[4], 71), 0)
    return {"documents": documents, "centroids": centroids, "candidates": candidates, "counts": counts}


sharpness = 40.0
smoothing = 0.02
prior_weight = 0.05
epsilon = 1e-06

def to_unit(values):
    as_float = values.astype(jnp.float32)
    inv_norm = lax.rsqrt(lax.optimization_barrier(jnp.mean(as_float * as_float, axis=-1, keepdims=True)) + epsilon)
    return (as_float * inv_norm / math.sqrt(values.shape[-1])).astype(jnp.bfloat16)

def reference(documents, centroids, candidates, counts):
    per_device = ROWS_DEV // BLOCK
    width_slots = SHARDS * SLOTS
    docs_unit = to_unit(documents).reshape(NBLK, BLOCK, E)
    cent_unit = to_unit(centroids)
    cent_float = cent_unit.astype(jnp.float32)
    listed = candidates.reshape(NBLK, SHARDS, SLOTS) + (jnp.arange(SHARDS, dtype=jnp.int32) * GROUPS_DEV)[None, :, None]
    listed = listed.reshape(NBLK, width_slots).astype(jnp.int32)
    live_slot = (jnp.arange(SLOTS, dtype=jnp.int32)[None, None, :] < counts[:, :, None]).reshape(NBLK, width_slots)

    def score_block(pieces):
        block_docs, block_groups, block_live = pieces
        cosine = jnp.einsum('de,ske->dsk', block_docs.astype(jnp.float32), cent_float[block_groups])
        return jnp.where(block_live[None, :, None], jnp.exp(sharpness * (cosine - 1.0)), jnp.float32(0.0))
    kernel = lax.map(score_block, (docs_unit, listed, live_slot))
    target = DOCS / CENTROIDS

    def scaled_rows(column):
        chosen = column[listed]
        return (chosen, 1.0 / jnp.einsum('bdsk,bsk->bd', kernel, chosen))
    column = jnp.ones((GROUPS, GROUP), jnp.float32)
    chosen, row_scale = scaled_rows(column)
    for sweep_index in range(PASSES):
        col_part = jnp.einsum('bdsk,bd->bsk', kernel, row_scale)
        column_total = jax.ops.segment_sum(col_part.reshape(-1, GROUP), listed.reshape(-1), num_segments=GROUPS)
        column = target / (column_total + smoothing)
        chosen, row_scale = scaled_rows(column)
    transport = (row_scale[:, :, None, None] * kernel * chosen[:, None, :, :]).astype(jnp.bfloat16)

    def device_sum(running, pieces):
        dev_plan, dev_docs, dev_groups = pieces

        def add_block(partial_value, block_pieces):
            blk_plan, blk_docs, blk_groups = block_pieces
            contrib = jnp.einsum('dsk,de->ske', blk_plan.astype(jnp.float32), blk_docs.astype(jnp.float32))
            return (partial_value.at[blk_groups].add(contrib), None)
        partial_value, unused = lax.scan(add_block, jnp.zeros((GROUPS, GROUP, E), jnp.float32), (dev_plan, dev_docs, dev_groups))
        rounded = lax.optimization_barrier(partial_value.astype(jnp.bfloat16))
        return (running + rounded.astype(jnp.float32), None)
    summed, unused = lax.scan(device_sum, jnp.zeros((GROUPS, GROUP, E), jnp.float32), (transport.reshape(N_DOC, per_device, BLOCK, width_slots, GROUP), docs_unit.reshape(N_DOC, per_device, BLOCK, E), listed.reshape(N_DOC, per_device, width_slots)))
    merged = summed + prior_weight * cent_float
    as_float = centroids.astype(jnp.float32)
    rescale = jnp.sqrt(lax.optimization_barrier(jnp.mean(as_float * as_float, axis=-1, keepdims=True))) * lax.rsqrt(lax.optimization_barrier(jnp.mean(merged * merged, axis=-1, keepdims=True)) + epsilon)
    return (merged * rescale).astype(jnp.bfloat16)
```

```python
import functools
import math

import jax
import jax.numpy as jnp
from jax import lax
from jax.experimental import pallas as pl
from jax.experimental.pallas import tpu as pltpu
from jax.sharding import PartitionSpec as P

BLOCK = 128
PASSES = 3
SIDE = 4

sharpness = 40.0
smoothing = 0.02
prior_weight = 0.05
epsilon = 1e-06

F32 = jnp.float32
BF16 = jnp.bfloat16
MESH = pl.DeviceIdType.MESH


def kernel(
    n_doc,
    n_cent,
    target,
    cand_ref,
    count_ref,
    place_ref,
    docs_hbm,
    cents_hbm,
    out_ref,
    docs,
    cents,
    own_raw,
    own_prior,
    own_rms,
    own_col,
    col_turned,
    kt,
    row_scale,
    column,
    row_send,
    row_recv,
    col_send,
    col_recv,
    parts,
    far_recv,
    near_recv,
    halfway,
    far_recv2,
    near_recv2,
    load_sems,
    row_send_sems,
    row_recv_sems,
    col_send_sems,
    col_recv_sems,
    far_sems,
    near_sems,
    far2_sems,
    near2_sems,
    sent_sems,
    sent2_sems,
):
    blocks, slots = cand_ref.shape
    groups, group_size, width = cents.shape
    half = width // 2
    d = lax.axis_index("doc")
    c = lax.axis_index("cent")
    x = lax.rem(d, SIDE)
    y = lax.div(d, SIDE)

    doc_step = docs.shape[0] // 4
    cent_step = groups // 8
    doc_loads = [
        pltpu.make_async_copy(
            docs_hbm.at[pl.ds(n * doc_step, doc_step)],
            docs.at[pl.ds(n * doc_step, doc_step)],
            load_sems.at[n],
        )
        for n in range(4)
    ]
    cent_loads = [
        pltpu.make_async_copy(
            cents_hbm.at[pl.ds(n * cent_step, cent_step)],
            cents.at[pl.ds(n * cent_step, cent_step)],
            load_sems.at[4 + n],
        )
        for n in range(8)
    ]
    own_pair = lax.div(d, 2)
    own_load = pltpu.make_async_copy(
        cents_hbm.at[:, pl.ds(pl.multiple_of(own_pair * 16, 16), 16)], own_raw, load_sems.at[12]
    )
    for copy in doc_loads + cent_loads + [own_load]:
        copy.start()

    barrier = pltpu.get_barrier_semaphore()
    for j in range(1, n_doc):
        pl.semaphore_signal(
            barrier, inc=1, device_id=(lax.rem(d + j, n_doc), c), device_id_type=MESH
        )
    for j in range(1, n_cent):
        pl.semaphore_signal(
            barrier, inc=1, device_id=(d, lax.rem(c + j, n_cent)), device_id_type=MESH
        )

    def unit(values):
        values = values.astype(F32)
        inv = lax.rsqrt(jnp.sum(values * values, axis=-1, keepdims=True) / width + epsilon)
        return values * (inv / math.sqrt(width))

    rows_at_once = 32

    def unit_docs(n, carry):
        at = pl.ds(pl.multiple_of(n * rows_at_once, rows_at_once), rows_at_once)
        docs[at, :] = unit(docs[at, :]).astype(BF16)
        return carry

    def unit_cents(n, carry):
        for m in range(group_size // rows_at_once):
            at = pl.ds(m * rows_at_once, rows_at_once)
            cents[n, at, :] = unit(cents[n, at, :]).astype(BF16)
        return carry

    for n in range(4):
        doc_loads[n].wait()
        per = doc_step // rows_at_once
        lax.fori_loop(n * per, (n + 1) * per, unit_docs, 0)
    for n in range(8):
        cent_loads[n].wait()
        lax.fori_loop(n * cent_step, (n + 1) * cent_step, unit_cents, 0)

    scale = sharpness * math.log2(math.e)

    def score(b, carry):
        at = pl.ds(pl.multiple_of(b * BLOCK, BLOCK), BLOCK)
        picked = jnp.concatenate([cents[cand_ref[b, s]] for s in range(slots)], axis=0)
        cosine = lax.dot_general(
            picked, docs[at, :], (((1,), (1,)), ((), ())), preferred_element_type=F32
        )
        total = jnp.zeros((1, BLOCK), F32)
        for s in range(slots):
            shift = jnp.where(s < count_ref[b, 0], F32(-scale), F32(-1e30))
            tile = jnp.exp2(cosine[s * group_size : (s + 1) * group_size] * scale + shift)
            total = total + jnp.sum(tile, axis=0, keepdims=True)
            kt[b * slots + s] = tile.astype(BF16)
        row_scale[pl.ds(b, 1), :] = total
        return carry

    lax.fori_loop(0, blocks, score, 0)
    kt[blocks * slots] = jnp.zeros((group_size, BLOCK), BF16)

    pl.semaphore_wait(barrier, n_doc - 1 + n_cent - 1)

    def send_rows(n, value):
        row_send[n] = value.astype(row_send.dtype)
        for j in range(1, n_cent):
            pltpu.make_async_remote_copy(
                src_ref=row_send.at[n],
                dst_ref=row_recv.at[n, j - 1],
                send_sem=row_send_sems.at[n],
                recv_sem=row_recv_sems.at[n],
                device_id=(d, lax.rem(c + j, n_cent)),
                device_id_type=MESH,
            ).start()

    def finish_rows(n):
        whole = row_recv.at[n]
        pltpu.make_async_copy(whole, whole, row_recv_sems.at[n]).wait()
        total = row_send[n].astype(F32)
        for j in range(n_cent - 1):
            total = total + row_recv[n, j].astype(F32)
        row_scale[...] = 1.0 / total

    def send_cols(n, value):
        col_send[n] = value.astype(col_send.dtype)
        for j in range(1, n_doc):
            pltpu.make_async_remote_copy(
                src_ref=col_send.at[n],
                dst_ref=col_recv.at[n, j - 1],
                send_sem=col_send_sems.at[n],
                recv_sem=col_recv_sems.at[n],
                device_id=(lax.rem(d + j, n_doc), c),
                device_id_type=MESH,
            ).start()

    def finish_cols(n):
        whole = col_recv.at[n]
        pltpu.make_async_copy(whole, whole, col_recv_sems.at[n]).wait()
        total = col_send[n].astype(F32)
        for j in range(n_doc - 1):
            total = total + col_recv[n, j].astype(F32)
        column[...] = target / (total + smoothing)

    def row_sums():
        row_index = lax.broadcasted_iota(jnp.int32, (blocks, BLOCK), 0)

        def add(b, total):
            pieces = [
                jnp.where(row_index == b, column[pl.ds(cand_ref[b, s], 1), :], 0.0).astype(BF16)
                for s in range(slots)
            ]
            left = jnp.concatenate(pieces, axis=1)
            right = jnp.concatenate([kt[b * slots + s] for s in range(slots)], axis=0)
            return total + jnp.dot(left, right, preferred_element_type=F32)

        return lax.fori_loop(0, blocks, add, jnp.zeros((blocks, BLOCK), F32))

    def col_sums():
        group_index = lax.broadcasted_iota(jnp.int32, (groups, BLOCK), 0)

        def add(b, total):
            row = row_scale[pl.ds(b, 1), :]
            pieces = [
                jnp.where(group_index == cand_ref[b, s], row, 0.0).astype(BF16)
                for s in range(slots)
            ]
            left = jnp.concatenate(pieces, axis=1)
            right = jnp.concatenate([kt[b * slots + s] for s in range(slots)], axis=1)
            return total + lax.dot_general(
                left, right, (((1,), (1,)), ((), ())), preferred_element_type=F32
            )

        return lax.fori_loop(0, blocks, add, jnp.zeros((groups, group_size), F32))

    send_rows(0, row_scale[...])

    own_load.wait()
    odd = lax.rem(d, 2) == 1

    def own_share(g, carry):
        raw = own_raw[g].astype(F32)
        raw = jnp.where(odd, raw[8:], raw[:8])
        mean = jnp.sum(raw * raw, axis=-1, keepdims=True) / width
        inv = lax.rsqrt(mean + epsilon) / math.sqrt(width)
        rounded = (raw * inv).astype(BF16).astype(F32)
        own_prior[g] = prior_weight * rounded
        own_rms[g] = jnp.broadcast_to(jnp.sqrt(mean), (8, 128))
        return carry

    lax.fori_loop(0, groups, own_share, 0)
    finish_rows(0)

    def sweep(n, carry):
        send_cols(n, col_sums())
        finish_cols(n)
        send_rows(n + 1, row_sums())

        @pl.when(n == PASSES - 1)
        def turn():
            padded = jnp.concatenate(
                [column[...], jnp.zeros((128 - groups, group_size), F32)], axis=0
            )
            col_turned[...] = padded.T
            mine = col_turned[pl.ds(pl.multiple_of(d * 8, 8), 8), :]
            for g in range(groups):
                own_col[g] = jnp.broadcast_to(mine[:, g : g + 1], (8, 128))

        finish_rows(n + 1)
        return carry

    lax.fori_loop(0, PASSES, sweep, 0)

    at_x = [y * SIDE + lax.rem(x + j, SIDE) for j in range(SIDE)]
    at_y = [lax.rem(y + j, SIDE) * SIDE + x for j in range(SIDE)]
    rounds = groups // 4

    def copy_to(doc, src, dst, send_sem, recv_sem):
        pltpu.make_async_remote_copy(
            src_ref=src,
            dst_ref=dst,
            send_sem=send_sem,
            recv_sem=recv_sem,
            device_id=(doc, c),
            device_id_type=MESH,
        ).start()

    def ring(q, second):
        along_x = (q == 0) != second
        places, pos = (at_x, x) if along_x else (at_y, y)
        right, left = places[1], places[3]
        return (
            right,
            left,
            pos,
            lax.rem(pos + 1, SIDE),
            lax.rem(pos + 2, SIDE),
            lax.rem(pos + 3, SIDE),
        )

    def weigh(u, q):
        p = 2 * u + q
        pieces = []
        for gg in range(2):
            pieces.append(
                jnp.concatenate(
                    [
                        (kt[place_ref[b, 2 * p + gg]].astype(F32) * row_scale[b : b + 1, :]).astype(
                            BF16
                        )
                        for b in range(blocks)
                    ],
                    axis=1,
                )
            )
        left = jnp.concatenate(pieces, axis=0)
        total = jnp.dot(left, docs[...], preferred_element_type=F32)
        for dest in range(n_doc):
            dy, dx = dest // SIDE, dest % SIDE
            first, then = (dx, dy) if q == 0 else (dy, dx)
            rows = jnp.concatenate(
                [
                    total[gg * group_size + 8 * dest : gg * group_size + 8 * dest + 8]
                    for gg in range(2)
                ],
                axis=0,
            ).astype(BF16)
            parts[p, first, 0, then] = rows[:, :half]
            parts[p, first, 1, then] = rows[:, half:]

    def leg_start(p, q, second):
        right, left, pos, near, far, back = ring(q, second)
        if second:
            piece = lambda place, h: halfway.at[p, h, place]
            far_to, near_to = far_recv2, near_recv2
            far_sem, near_sem, sent = far2_sems.at[p], near2_sems.at[p], sent2_sems.at[p]
        else:
            piece = lambda place, h: parts.at[p, place, h]
            far_to, near_to = far_recv, near_recv
            far_sem, near_sem, sent = far_sems.at[p], near_sems.at[p], sent_sems.at[p]
        copy_to(right, piece(far, 0), far_to.at[p, 0], sent, far_sem)
        copy_to(left, piece(far, 1), far_to.at[p, 1], sent, far_sem)
        copy_to(right, piece(near, 1), near_to.at[p, 0, 1], sent, near_sem)
        copy_to(left, piece(back, 0), near_to.at[p, 1, 0], sent, near_sem)

    def leg_relay(p, q, second):
        right, left, pos, near, far, back = ring(q, second)
        if second:
            got, near_to = far_recv2, near_recv2
            far_sem, near_sem, sent = far2_sems.at[p], near2_sems.at[p], sent2_sems.at[p]
        else:
            got, near_to = far_recv, near_recv
            far_sem, near_sem, sent = far_sems.at[p], near_sems.at[p], sent_sems.at[p]
        whole = got.at[p]
        pltpu.make_async_copy(whole, whole, far_sem).wait()
        for h, place, device in ((0, near, right), (1, back, left)):
            if second:
                halfway[p, h, place] = (
                    halfway[p, h, place].astype(F32) + got[p, h].astype(F32)
                ).astype(BF16)
                src = halfway.at[p, h, place]
            else:
                parts[p, place, h] = (
                    parts[p, place, h].astype(F32) + got[p, h].astype(F32)
                ).astype(BF16)
                src = parts.at[p, place, h]
            copy_to(device, src, near_to.at[p, h, h], sent, near_sem)

    def leg_end(p, q, second):
        pos = ring(q, second)[2]
        if second:
            whole = near_recv2.at[p]
            pltpu.make_async_copy(whole, whole, near2_sems.at[p]).wait()
            return [
                halfway[p, h, pos].astype(F32)
                + near_recv2[p, 0, h].astype(F32)
                + near_recv2[p, 1, h].astype(F32)
                for h in range(2)
            ]
        whole = near_recv.at[p]
        pltpu.make_async_copy(whole, whole, near_sems.at[p]).wait()
        for h in range(2):
            halfway[p, h] = (
                parts[p, pos, h].astype(F32)
                + near_recv[p, 0, h].astype(F32)
                + near_recv[p, 1, h].astype(F32)
            ).astype(BF16)

    def finish(p, sums):
        for gg in range(2):
            g = 2 * p + gg
            weight = own_col[g][:, :1]
            prior = own_prior[g]
            low = sums[0][8 * gg : 8 * gg + 8] * weight + prior[:, :half]
            high = sums[1][8 * gg : 8 * gg + 8] * weight + prior[:, half:]
            square = jnp.sum(low * low, axis=-1, keepdims=True) + jnp.sum(
                high * high, axis=-1, keepdims=True
            )
            rescale = own_rms[g][:, :1] * lax.rsqrt(square / width + epsilon)
            out_ref[g, :, :half] = (low * rescale).astype(BF16)
            out_ref[g, :, half:] = (high * rescale).astype(BF16)

    def turn_of(u, carry):
        @pl.when(u < rounds)
        def _():
            for q in range(2):
                weigh(u, q)
                leg_start(2 * u + q, q, False)

        @pl.when((u >= 1) & (u < rounds + 1))
        def _():
            for q in range(2):
                leg_relay(2 * (u - 1) + q, q, False)

        @pl.when((u >= 2) & (u < rounds + 2))
        def _():
            for q in range(2):
                p = 2 * (u - 2) + q
                leg_end(p, q, False)
                leg_start(p, q, True)

        @pl.when((u >= 3) & (u < rounds + 3))
        def _():
            for q in range(2):
                leg_relay(2 * (u - 3) + q, q, True)

        @pl.when(u >= 4)
        def _():
            for q in range(2):
                p = 2 * (u - 4) + q
                finish(p, leg_end(p, q, True))

        return carry

    lax.fori_loop(0, rounds + 4, turn_of, 0)

    def sent(p, carry):
        whole = parts.at[p, pl.ds(0, 3)]
        pltpu.make_async_copy(whole, whole, sent_sems.at[p]).wait()
        whole = halfway.at[p, :, pl.ds(0, 3)]
        pltpu.make_async_copy(whole, whole, sent2_sems.at[p]).wait()
        return carry

    lax.fori_loop(0, 2 * rounds, sent, 0)
    for n in range(PASSES + 1):
        whole = row_recv.at[n]
        pltpu.make_async_copy(whole, whole, row_send_sems.at[n]).wait()
    for n in range(PASSES):
        whole = col_recv.at[n]
        pltpu.make_async_copy(whole, whole, col_send_sems.at[n]).wait()


def body(n_doc, n_cent, documents, centroids, candidates, counts):
    rows_dev, width = documents.shape
    groups, group_size, unused_width = centroids.shape
    blocks, slots = candidates.shape
    half = width // 2
    pairs = groups // 2
    target = rows_dev * n_doc / (groups * group_size * n_cent)
    slot = jnp.arange(slots, dtype=jnp.int32)
    flat = jnp.arange(blocks, dtype=jnp.int32)[:, None] * slots + slot[None, :]
    flat = jnp.where(slot[None, :] < counts, flat, blocks * slots)
    names = candidates[:, :, None] == jnp.arange(groups, dtype=jnp.int32)[None, None, :]
    place = jnp.min(jnp.where(names, flat[:, :, None], blocks * slots), axis=1)
    dma = pltpu.SemaphoreType.DMA
    return pl.pallas_call(
        functools.partial(kernel, n_doc, n_cent, target),
        out_shape=jax.ShapeDtypeStruct((groups, group_size // n_doc, width), BF16),
        in_specs=[pl.BlockSpec(memory_space=pltpu.SMEM)] * 3
        + [pl.BlockSpec(memory_space=pl.ANY)] * 2,
        out_specs=pl.BlockSpec(memory_space=pltpu.VMEM),
        scratch_shapes=[
            pltpu.VMEM((rows_dev, width), BF16),
            pltpu.VMEM((groups, group_size, width), BF16),
            pltpu.VMEM((groups, 16, width), BF16),
            pltpu.VMEM((groups, 8, width), F32),
            pltpu.VMEM((groups, 8, 128), F32),
            pltpu.VMEM((groups, 8, 128), F32),
            pltpu.VMEM((128, 128), F32),
            pltpu.VMEM((blocks * slots + 1, group_size, BLOCK), BF16),
            pltpu.VMEM((blocks, BLOCK), F32),
            pltpu.VMEM((groups, group_size), F32),
            pltpu.VMEM((PASSES + 1, blocks, BLOCK), BF16),
            pltpu.VMEM((PASSES + 1, n_cent - 1, blocks, BLOCK), BF16),
            pltpu.VMEM((PASSES, groups, group_size), BF16),
            pltpu.VMEM((PASSES, n_doc - 1, groups, group_size), BF16),
            pltpu.VMEM((pairs, SIDE, 2, SIDE, 16, half), BF16),
            pltpu.VMEM((pairs, 2, SIDE, 16, half), BF16),
            pltpu.VMEM((pairs, 2, 2, SIDE, 16, half), BF16),
            pltpu.VMEM((pairs, 2, SIDE, 16, half), BF16),
            pltpu.VMEM((pairs, 2, 16, half), BF16),
            pltpu.VMEM((pairs, 2, 2, 16, half), BF16),
            dma((13,)),
            dma((PASSES + 1,)),
            dma((PASSES + 1,)),
            dma((PASSES,)),
            dma((PASSES,)),
            dma((pairs,)),
            dma((pairs,)),
            dma((pairs,)),
            dma((pairs,)),
            dma((pairs,)),
            dma((pairs,)),
        ],
        compiler_params=pltpu.CompilerParams(
            collective_id=0, has_side_effects=True, vmem_limit_bytes=56 * 1024 * 1024
        ),
    )(candidates, counts, place, documents, centroids)


def solution(mesh):
    n_doc, n_cent = mesh.shape["doc"], mesh.shape["cent"]
    return jax.shard_map(
        functools.partial(body, n_doc, n_cent),
        mesh=mesh,
        in_specs=(P("doc", None), P("cent", None, None), P("doc", "cent"), P("doc", "cent")),
        out_specs=P("cent", "doc", None),
        check_vma=False,
    )
```

```python
import functools
import math

import jax
import jax.numpy as jnp
from jax import lax
from jax.experimental import pallas as pl
from jax.experimental.pallas import tpu as pltpu
from jax.sharding import PartitionSpec as P

BLOCK = 128
PASSES = 3
SIDE = 4
LAGS = (0, 2, 4, 6, 8)

sharpness = 40.0
smoothing = 0.02
prior_weight = 0.05
epsilon = 1e-06

F32 = jnp.float32
BF16 = jnp.bfloat16
MESH = pl.DeviceIdType.MESH


def kernel(
    n_doc,
    n_cent,
    target,
    names_ref,
    live_ref,
    names_rows,
    live_rows,
    docs_hbm,
    cents_hbm,
    out_ref,
    docs,
    cents,
    own_raw,
    own_prior,
    own_rms,
    own_col,
    col_turned,
    kt,
    row_scale,
    column,
    row_send,
    row_recv,
    col_send,
    col_recv,
    parts,
    far_recv,
    near_recv,
    halfway,
    far_recv2,
    near_recv2,
    place_rows,
    place_ref,
    load_sems,
    row_send_sems,
    row_recv_sems,
    col_send_sems,
    col_recv_sems,
    far_sems,
    near_sems,
    far2_sems,
    near2_sems,
    sent_sems,
    sent2_sems,
):
    groups, group_size, width = cents.shape
    slots, blocks = names_ref.shape

    def cand(b, s):
        return names_ref[s, b]

    def count(b):
        return live_ref[0, b]

    def place(b, g):
        return place_ref[g, b]

    half = width // 2
    d = lax.axis_index("doc")
    c = lax.axis_index("cent")
    x = lax.rem(d, SIDE)
    y = lax.div(d, SIDE)

    doc_step = docs.shape[0] // 4
    cent_step = groups // 8
    doc_loads = [
        pltpu.make_async_copy(
            docs_hbm.at[pl.ds(n * doc_step, doc_step)],
            docs.at[pl.ds(n * doc_step, doc_step)],
            load_sems.at[n],
        )
        for n in range(4)
    ]
    cent_loads = [
        pltpu.make_async_copy(
            cents_hbm.at[pl.ds(n * cent_step, cent_step)],
            cents.at[pl.ds(n * cent_step, cent_step)],
            load_sems.at[4 + n],
        )
        for n in range(8)
    ]
    own_pair = lax.div(d, 2)
    own_load = pltpu.make_async_copy(
        cents_hbm.at[:, pl.ds(pl.multiple_of(own_pair * 16, 16), 16)], own_raw, load_sems.at[12]
    )
    for copy in cent_loads + doc_loads + [own_load]:
        copy.start()

    zero_tile = blocks * slots
    group_index = lax.broadcasted_iota(jnp.int32, (groups, blocks), 0)
    block_index = lax.broadcasted_iota(jnp.int32, (groups, blocks), 1)
    tiles = jnp.full((groups, blocks), zero_tile, jnp.int32)
    for s in range(slots):
        named = (names_rows[s : s + 1, :] == group_index) & (live_rows[...] > s)
        tiles = jnp.where(named, block_index * slots + s, tiles)
    place_rows[:, :blocks] = tiles
    place_copy = pltpu.make_async_copy(place_rows, place_ref, load_sems.at[13])
    place_copy.start()

    barrier = pltpu.get_barrier_semaphore()
    for j in range(1, n_doc):
        pl.semaphore_signal(
            barrier, inc=1, device_id=(lax.rem(d + j, n_doc), c), device_id_type=MESH
        )
    for j in range(1, n_cent):
        pl.semaphore_signal(
            barrier, inc=1, device_id=(d, lax.rem(c + j, n_cent)), device_id_type=MESH
        )

    def unit(values):
        values = values.astype(F32)
        inv = lax.rsqrt(jnp.sum(values * values, axis=-1, keepdims=True) / width + epsilon)
        return values * (inv / math.sqrt(width))

    def unit_cents(n, carry):
        at = pl.ds(n * cent_step, cent_step)
        cents[at] = unit(cents[at]).astype(BF16)
        return carry

    for n in range(8):
        cent_loads[n].wait()
        lax.fori_loop(n, n + 1, unit_cents, 0)
    for n in range(4):
        doc_loads[n].wait()

    scale = sharpness * math.log2(math.e)

    def score(b, carry):
        at = pl.ds(pl.multiple_of(b * BLOCK, BLOCK), BLOCK)
        rows = unit(docs[at, :]).astype(BF16)
        docs[at, :] = rows
        picked = jnp.concatenate([cents[cand(b, s)] for s in range(slots)], axis=0)
        cosine = lax.dot_general(
            picked, rows, (((1,), (1,)), ((), ())), preferred_element_type=F32
        )
        total = jnp.zeros((8, BLOCK), F32)
        for s in range(slots):
            shift = jnp.where(s < count(b), F32(-scale), F32(-1e30))
            tile = jnp.exp2(cosine[s * group_size : (s + 1) * group_size] * scale + shift)
            total = total + jnp.sum(tile.reshape(group_size // 8, 8, BLOCK), axis=0)
            kt[b * slots + s] = tile.astype(BF16)
        row_scale[pl.ds(b, 1), :] = jnp.sum(total, axis=0, keepdims=True)
        return carry

    lax.fori_loop(0, blocks, score, 0, unroll=min(4, blocks))
    kt[blocks * slots] = jnp.zeros((group_size, BLOCK), BF16)

    pl.semaphore_wait(barrier, n_doc - 1 + n_cent - 1)

    def send_rows(n, value):
        row_send[n] = value.astype(row_send.dtype)
        for j in sorted(range(1, n_cent), key=lambda j: -min(j // 2, n_cent // 2 - j // 2)):
            pltpu.make_async_remote_copy(
                src_ref=row_send.at[n],
                dst_ref=row_recv.at[n, j - 1],
                send_sem=row_send_sems.at[n],
                recv_sem=row_recv_sems.at[n],
                device_id=(d, lax.rem(c + j, n_cent)),
                device_id_type=MESH,
            ).start()

    def finish_rows(n):
        whole = row_recv.at[n]
        pltpu.make_async_copy(whole, whole, row_recv_sems.at[n]).wait()
        total = row_send[n].astype(F32)
        for j in range(n_cent - 1):
            total = total + row_recv[n, j].astype(F32)
        row_scale[...] = 1.0 / total

    def send_cols(n, value):
        col_send[n] = value.astype(col_send.dtype)
        for j in sorted(range(1, n_doc), key=lambda j: -(2 - abs(2 - j % 4) + 2 - abs(2 - j // 4))):
            pltpu.make_async_remote_copy(
                src_ref=col_send.at[n],
                dst_ref=col_recv.at[n, j - 1],
                send_sem=col_send_sems.at[n],
                recv_sem=col_recv_sems.at[n],
                device_id=(lax.rem(d + j, n_doc), c),
                device_id_type=MESH,
            ).start()

    def finish_cols(n):
        whole = col_recv.at[n]
        pltpu.make_async_copy(whole, whole, col_recv_sems.at[n]).wait()
        total = col_send[n].astype(F32)
        for j in range(n_doc - 1):
            total = total + col_recv[n, j].astype(F32)
        column[...] = target / (total + smoothing)

    def row_sums():
        row_index = lax.broadcasted_iota(jnp.int32, (blocks, BLOCK), 0)

        def add(b, total):
            pieces = [
                jnp.where(row_index == b, column[pl.ds(cand(b, s), 1), :], 0.0).astype(BF16)
                for s in range(slots)
            ]
            left = jnp.concatenate(pieces, axis=1)
            right = jnp.concatenate([kt[b * slots + s] for s in range(slots)], axis=0)
            return total + jnp.dot(left, right, preferred_element_type=F32)

        return lax.fori_loop(0, blocks, add, jnp.zeros((blocks, BLOCK), F32), unroll=blocks)

    def col_sums():
        group_index = lax.broadcasted_iota(jnp.int32, (groups, BLOCK), 0)

        def add(b, total):
            row = row_scale[pl.ds(b, 1), :]
            pieces = [
                jnp.where(group_index == cand(b, s), row, 0.0).astype(BF16)
                for s in range(slots)
            ]
            left = jnp.concatenate(pieces, axis=1)
            right = jnp.concatenate([kt[b * slots + s] for s in range(slots)], axis=1)
            return total + lax.dot_general(
                left, right, (((1,), (1,)), ((), ())), preferred_element_type=F32
            )

        return lax.fori_loop(0, blocks, add, jnp.zeros((groups, group_size), F32), unroll=blocks)

    send_rows(0, row_scale[...])

    own_load.wait()
    place_copy.wait()
    odd = lax.rem(d, 2) == 1

    def own_share(g, carry):
        raw = own_raw[g].astype(F32)
        raw = jnp.where(odd, raw[8:], raw[:8])
        mean = jnp.sum(raw * raw, axis=-1, keepdims=True) / width
        inv = lax.rsqrt(mean + epsilon) / math.sqrt(width)
        rounded = (raw * inv).astype(BF16).astype(F32)
        own_prior[g] = prior_weight * rounded
        own_rms[g] = jnp.broadcast_to(jnp.sqrt(mean), (8, 128))
        return carry

    lax.fori_loop(0, groups, own_share, 0)
    finish_rows(0)

    def sweep(n, carry):
        send_cols(n, col_sums())
        finish_cols(n)
        send_rows(n + 1, row_sums())

        @pl.when(n == PASSES - 1)
        def turn():
            padded = jnp.concatenate(
                [column[...], jnp.zeros((128 - groups, group_size), F32)], axis=0
            )
            col_turned[...] = padded.T
            mine = col_turned[pl.ds(pl.multiple_of(d * 8, 8), 8), :]
            for g in range(groups):
                own_col[g] = jnp.broadcast_to(mine[:, g : g + 1], (8, 128))

        finish_rows(n + 1)
        return carry

    lax.fori_loop(0, PASSES, sweep, 0)

    at_x = [y * SIDE + lax.rem(x + j, SIDE) for j in range(SIDE)]
    at_y = [lax.rem(y + j, SIDE) * SIDE + x for j in range(SIDE)]
    rounds = groups // 4

    def copy_to(doc, src, dst, send_sem, recv_sem):
        pltpu.make_async_remote_copy(
            src_ref=src,
            dst_ref=dst,
            send_sem=send_sem,
            recv_sem=recv_sem,
            device_id=(doc, c),
            device_id_type=MESH,
        ).start()

    def ring(q, second):
        along_x = (q == 0) != second
        places, pos = (at_x, x) if along_x else (at_y, y)
        right, left = places[1], places[3]
        return (
            right,
            left,
            pos,
            lax.rem(pos + 1, SIDE),
            lax.rem(pos + 2, SIDE),
            lax.rem(pos + 3, SIDE),
        )

    def weigh(p, q):
        pieces = []
        for gg in range(2):
            pieces.append(
                jnp.concatenate(
                    [
                        (kt[place(b, 2 * p + gg)].astype(F32) * row_scale[b : b + 1, :]).astype(
                            BF16
                        )
                        for b in range(blocks)
                    ],
                    axis=1,
                )
            )
        left = jnp.concatenate(pieces, axis=0)
        total = jnp.dot(left, docs[...], preferred_element_type=F32)
        for dest in range(n_doc):
            dy, dx = dest // SIDE, dest % SIDE
            first, then = (dx, dy) if q == 0 else (dy, dx)
            rows = jnp.concatenate(
                [
                    total[gg * group_size + 8 * dest : gg * group_size + 8 * dest + 8]
                    for gg in range(2)
                ],
                axis=0,
            ).astype(BF16)
            parts[p, first, 0, then] = rows[:, :half]
            parts[p, first, 1, then] = rows[:, half:]

    def leg_start(p, q, second):
        right, left, pos, near, far, back = ring(q, second)
        if second:
            piece = lambda place, h: halfway.at[p, h, place]
            far_to, near_to = far_recv2, near_recv2
            far_sem, near_sem, sent = far2_sems.at[p], near2_sems.at[p], sent2_sems.at[p]
        else:
            piece = lambda place, h: parts.at[p, place, h]
            far_to, near_to = far_recv, near_recv
            far_sem, near_sem, sent = far_sems.at[p], near_sems.at[p], sent_sems.at[p]
        copy_to(right, piece(far, 0), far_to.at[p, 0], sent, far_sem)
        copy_to(left, piece(far, 1), far_to.at[p, 1], sent, far_sem)
        copy_to(right, piece(near, 1), near_to.at[p, 0, 1], sent, near_sem)
        copy_to(left, piece(back, 0), near_to.at[p, 1, 0], sent, near_sem)

    def leg_relay(p, q, second):
        right, left, pos, near, far, back = ring(q, second)
        if second:
            got, near_to = far_recv2, near_recv2
            far_sem, near_sem, sent = far2_sems.at[p], near2_sems.at[p], sent2_sems.at[p]
        else:
            got, near_to = far_recv, near_recv
            far_sem, near_sem, sent = far_sems.at[p], near_sems.at[p], sent_sems.at[p]
        whole = got.at[p]
        pltpu.make_async_copy(whole, whole, far_sem).wait()
        for h, place, device in ((0, near, right), (1, back, left)):
            if second:
                halfway[p, h, place] = (
                    halfway[p, h, place].astype(F32) + got[p, h].astype(F32)
                ).astype(BF16)
                src = halfway.at[p, h, place]
            else:
                parts[p, place, h] = (
                    parts[p, place, h].astype(F32) + got[p, h].astype(F32)
                ).astype(BF16)
                src = parts.at[p, place, h]
            copy_to(device, src, near_to.at[p, h, h], sent, near_sem)

    def leg_end(p, q, second):
        pos = ring(q, second)[2]
        if second:
            whole = near_recv2.at[p]
            pltpu.make_async_copy(whole, whole, near2_sems.at[p]).wait()
            return [
                halfway[p, h, pos].astype(F32)
                + near_recv2[p, 0, h].astype(F32)
                + near_recv2[p, 1, h].astype(F32)
                for h in range(2)
            ]
        whole = near_recv.at[p]
        pltpu.make_async_copy(whole, whole, near_sems.at[p]).wait()
        for h in range(2):
            halfway[p, h] = (
                parts[p, pos, h].astype(F32)
                + near_recv[p, 0, h].astype(F32)
                + near_recv[p, 1, h].astype(F32)
            ).astype(BF16)

    def finish(p, sums):
        for gg in range(2):
            g = 2 * p + gg
            weight = own_col[g][:, :1]
            prior = own_prior[g]
            low = sums[0][8 * gg : 8 * gg + 8] * weight + prior[:, :half]
            high = sums[1][8 * gg : 8 * gg + 8] * weight + prior[:, half:]
            square = jnp.sum(low * low, axis=-1, keepdims=True) + jnp.sum(
                high * high, axis=-1, keepdims=True
            )
            rescale = own_rms[g][:, :1] * lax.rsqrt(square / width + epsilon)
            out_ref[g, :, :half] = (low * rescale).astype(BF16)
            out_ref[g, :, half:] = (high * rescale).astype(BF16)

    pairs = 2 * rounds

    def turn_of(t, q):
        def begin(p, q):
            weigh(p, q)
            leg_start(p, q, False)

        def middle(p, q):
            leg_end(p, q, False)
            leg_start(p, q, True)

        stages = (
            begin,
            lambda p, q: leg_relay(p, q, False),
            middle,
            lambda p, q: leg_relay(p, q, True),
            lambda p, q: finish(p, leg_end(p, q, True)),
        )
        for lag, step in zip(LAGS, stages):
            p = t - lag

            @pl.when((p >= 0) & (p < pairs))
            def _(p=p, lag=lag, step=step):
                step(p, (q - lag) % 2)

    def two_turns(u, carry):
        for q in range(2):
            turn_of(2 * u + q, q)
        return carry

    lax.fori_loop(0, (pairs + LAGS[-1] + 1) // 2, two_turns, 0)

    def sent(p, carry):
        whole = parts.at[p, pl.ds(0, 3)]
        pltpu.make_async_copy(whole, whole, sent_sems.at[p]).wait()
        whole = halfway.at[p, :, pl.ds(0, 3)]
        pltpu.make_async_copy(whole, whole, sent2_sems.at[p]).wait()
        return carry

    lax.fori_loop(0, 2 * rounds, sent, 0)
    for n in range(PASSES + 1):
        whole = row_recv.at[n]
        pltpu.make_async_copy(whole, whole, row_send_sems.at[n]).wait()
    for n in range(PASSES):
        whole = col_recv.at[n]
        pltpu.make_async_copy(whole, whole, col_send_sems.at[n]).wait()


def body(n_doc, n_cent, documents, centroids, candidates, counts):
    rows_dev, width = documents.shape
    groups, group_size, unused_width = centroids.shape
    blocks, slots = candidates.shape
    half = width // 2
    pairs = groups // 2
    target = rows_dev * n_doc / (groups * group_size * n_cent)
    names = candidates.T
    live = counts.T
    dma = pltpu.SemaphoreType.DMA
    return pl.pallas_call(
        functools.partial(kernel, n_doc, n_cent, target),
        out_shape=jax.ShapeDtypeStruct((groups, group_size // n_doc, width), BF16),
        in_specs=[pl.BlockSpec(memory_space=pltpu.SMEM)] * 2
        + [pl.BlockSpec(memory_space=pltpu.VMEM)] * 2
        + [pl.BlockSpec(memory_space=pl.ANY)] * 2,
        out_specs=pl.BlockSpec(memory_space=pltpu.VMEM),
        scratch_shapes=[
            pltpu.VMEM((rows_dev, width), BF16),
            pltpu.VMEM((groups, group_size, width), BF16),
            pltpu.VMEM((groups, 16, width), BF16),
            pltpu.VMEM((groups, 8, width), F32),
            pltpu.VMEM((groups, 8, 128), F32),
            pltpu.VMEM((groups, 8, 128), F32),
            pltpu.VMEM((128, 128), F32),
            pltpu.VMEM((blocks * slots + 1, group_size, BLOCK), BF16),
            pltpu.VMEM((blocks, BLOCK), F32),
            pltpu.VMEM((groups, group_size), F32),
            pltpu.VMEM((PASSES + 1, blocks, BLOCK), BF16),
            pltpu.VMEM((PASSES + 1, n_cent - 1, blocks, BLOCK), BF16),
            pltpu.VMEM((PASSES, groups, group_size), BF16),
            pltpu.VMEM((PASSES, n_doc - 1, groups, group_size), BF16),
            pltpu.VMEM((pairs, SIDE, 2, SIDE, 16, half), BF16),
            pltpu.VMEM((pairs, 2, SIDE, 16, half), BF16),
            pltpu.VMEM((pairs, 2, 2, SIDE, 16, half), BF16),
            pltpu.VMEM((pairs, 2, SIDE, 16, half), BF16),
            pltpu.VMEM((pairs, 2, 16, half), BF16),
            pltpu.VMEM((pairs, 2, 2, 16, half), BF16),
            pltpu.VMEM((groups, 128), jnp.int32),
            pltpu.SMEM((groups, 128), jnp.int32),
            dma((14,)),
            dma((PASSES + 1,)),
            dma((PASSES + 1,)),
            dma((PASSES,)),
            dma((PASSES,)),
            dma((pairs,)),
            dma((pairs,)),
            dma((pairs,)),
            dma((pairs,)),
            dma((pairs,)),
            dma((pairs,)),
        ],
        compiler_params=pltpu.CompilerParams(
            collective_id=0, has_side_effects=True, vmem_limit_bytes=56 * 1024 * 1024
        ),
    )(names, live, names, live, documents, centroids)


def solution(mesh):
    n_doc, n_cent = mesh.shape["doc"], mesh.shape["cent"]
    return jax.shard_map(
        functools.partial(body, n_doc, n_cent),
        mesh=mesh,
        in_specs=(P("doc", None), P("cent", None, None), P("doc", "cent"), P("doc", "cent")),
        out_specs=P("cent", "doc", None),
        check_vma=False,
    )
```

```python
import functools
import math

import jax
import jax.numpy as jnp
from jax import lax
from jax.experimental import pallas as pl
from jax.experimental.pallas import tpu as pltpu
from jax.sharding import PartitionSpec as P

BLOCK = 128
PASSES = 3
SIDE = 4
ORDER = (0, 2, 1, 3, 4)
LAGS = (0, 3, 0, 7, 11)

sharpness = 40.0
smoothing = 0.02
prior_weight = 0.05
epsilon = 1e-06

F32 = jnp.float32
BF16 = jnp.bfloat16
MESH = pl.DeviceIdType.MESH


def kernel(
    n_doc,
    n_cent,
    target,
    names_ref,
    live_ref,
    names_rows,
    live_rows,
    docs_hbm,
    cents_hbm,
    out_ref,
    docs,
    cents,
    own_raw,
    own_prior,
    own_rms,
    own_col,
    col_turned,
    kt,
    row_scale,
    column,
    row_send,
    row_recv,
    col_send,
    col_recv,
    parts,
    far_recv,
    near_recv,
    halfway,
    last_recv,
    place_rows,
    place_ref,
    load_sems,
    row_send_sems,
    row_recv_sems,
    col_send_sems,
    col_recv_sems,
    far_sems,
    near_sems,
    last_sems,
    sent_sems,
    sent2_sems,
):
    groups, group_size, width = cents.shape
    slots, blocks = names_ref.shape

    def cand(b, s):
        return names_ref[s, b]

    def count(b):
        return live_ref[0, b]

    def place(b, g):
        return place_ref[g, b]

    half = width // 2
    d = lax.axis_index("doc")
    c = lax.axis_index("cent")
    x = lax.rem(d, SIDE)
    y = lax.div(d, SIDE)

    doc_step = docs.shape[0] // 4
    cent_step = groups // 8
    doc_loads = [
        pltpu.make_async_copy(
            docs_hbm.at[pl.ds(n * doc_step, doc_step)],
            docs.at[pl.ds(n * doc_step, doc_step)],
            load_sems.at[n],
        )
        for n in range(4)
    ]
    cent_loads = [
        pltpu.make_async_copy(
            cents_hbm.at[pl.ds(n * cent_step, cent_step)],
            cents.at[pl.ds(n * cent_step, cent_step)],
            load_sems.at[4 + n],
        )
        for n in range(8)
    ]
    own_pair = lax.div(d, 2)
    own_load = pltpu.make_async_copy(
        cents_hbm.at[:, pl.ds(pl.multiple_of(own_pair * 16, 16), 16)], own_raw, load_sems.at[12]
    )
    for copy in cent_loads + doc_loads + [own_load]:
        copy.start()

    zero_tile = blocks * slots
    group_index = lax.broadcasted_iota(jnp.int32, (groups, blocks), 0)
    block_index = lax.broadcasted_iota(jnp.int32, (groups, blocks), 1)
    tiles = jnp.full((groups, blocks), zero_tile, jnp.int32)
    for s in range(slots):
        named = (names_rows[s : s + 1, :] == group_index) & (live_rows[...] > s)
        tiles = jnp.where(named, block_index * slots + s, tiles)
    place_rows[:, :blocks] = tiles
    place_copy = pltpu.make_async_copy(place_rows, place_ref, load_sems.at[13])
    place_copy.start()

    barrier = pltpu.get_barrier_semaphore()
    for j in range(1, n_doc):
        pl.semaphore_signal(
            barrier, inc=1, device_id=(lax.rem(d + j, n_doc), c), device_id_type=MESH
        )
    for j in range(1, n_cent):
        pl.semaphore_signal(
            barrier, inc=1, device_id=(d, lax.rem(c + j, n_cent)), device_id_type=MESH
        )

    def unit(values):
        values = values.astype(F32)
        inv = lax.rsqrt(jnp.sum(values * values, axis=-1, keepdims=True) / width + epsilon)
        return values * (inv / math.sqrt(width))

    def unit_cents(n, carry):
        at = pl.ds(n * cent_step, cent_step)
        cents[at] = unit(cents[at]).astype(BF16)
        return carry

    for n in range(8):
        cent_loads[n].wait()
        lax.fori_loop(n, n + 1, unit_cents, 0)
    for n in range(4):
        doc_loads[n].wait()

    scale = sharpness * math.log2(math.e)

    def score(b, carry):
        at = pl.ds(pl.multiple_of(b * BLOCK, BLOCK), BLOCK)
        rows = unit(docs[at, :]).astype(BF16)
        docs[at, :] = rows
        picked = jnp.concatenate([cents[cand(b, s)] for s in range(slots)], axis=0)
        cosine = lax.dot_general(
            picked, rows, (((1,), (1,)), ((), ())), preferred_element_type=F32
        )
        total = jnp.zeros((8, BLOCK), F32)
        for s in range(slots):
            shift = jnp.where(s < count(b), F32(-scale), F32(-1e30))
            tile = jnp.exp2(cosine[s * group_size : (s + 1) * group_size] * scale + shift)
            total = total + jnp.sum(tile.reshape(group_size // 8, 8, BLOCK), axis=0)
            kt[b * slots + s] = tile.astype(BF16)
        row_scale[pl.ds(b, 1), :] = jnp.sum(total, axis=0, keepdims=True)
        return carry

    lax.fori_loop(0, blocks, score, 0, unroll=blocks)
    kt[blocks * slots] = jnp.zeros((group_size, BLOCK), BF16)

    pl.semaphore_wait(barrier, n_doc - 1 + n_cent - 1)

    def send_rows(n, value):
        row_send[n] = value.astype(row_send.dtype)
        for j in sorted(range(1, n_cent), key=lambda j: -min(j // 2, n_cent // 2 - j // 2)):
            pltpu.make_async_remote_copy(
                src_ref=row_send.at[n],
                dst_ref=row_recv.at[n, j - 1],
                send_sem=row_send_sems.at[n],
                recv_sem=row_recv_sems.at[n],
                device_id=(d, lax.rem(c + j, n_cent)),
                device_id_type=MESH,
            ).start()

    def finish_rows(n):
        whole = row_recv.at[n]
        pltpu.make_async_copy(whole, whole, row_recv_sems.at[n]).wait()
        total = row_send[n].astype(F32)
        for j in range(n_cent - 1):
            total = total + row_recv[n, j].astype(F32)
        row_scale[...] = 1.0 / total

    def send_cols(n, value):
        col_send[n] = value.astype(col_send.dtype)
        for j in sorted(range(1, n_doc), key=lambda j: -(2 - abs(2 - j % 4) + 2 - abs(2 - j // 4))):
            pltpu.make_async_remote_copy(
                src_ref=col_send.at[n],
                dst_ref=col_recv.at[n, j - 1],
                send_sem=col_send_sems.at[n],
                recv_sem=col_recv_sems.at[n],
                device_id=(lax.rem(d + j, n_doc), c),
                device_id_type=MESH,
            ).start()

    def finish_cols(n):
        whole = col_recv.at[n]
        pltpu.make_async_copy(whole, whole, col_recv_sems.at[n]).wait()
        total = col_send[n].astype(F32)
        for j in range(n_doc - 1):
            total = total + col_recv[n, j].astype(F32)
        column[...] = target / (total + smoothing)

    def row_sums():
        row_index = lax.broadcasted_iota(jnp.int32, (blocks, BLOCK), 0)

        def add(b, total):
            pieces = [
                jnp.where(row_index == b, column[pl.ds(cand(b, s), 1), :], 0.0).astype(BF16)
                for s in range(slots)
            ]
            left = jnp.concatenate(pieces, axis=1)
            right = jnp.concatenate([kt[b * slots + s] for s in range(slots)], axis=0)
            return total + jnp.dot(left, right, preferred_element_type=F32)

        return lax.fori_loop(0, blocks, add, jnp.zeros((blocks, BLOCK), F32), unroll=blocks)

    def col_sums():
        group_index = lax.broadcasted_iota(jnp.int32, (groups, BLOCK), 0)

        def add(b, total):
            row = row_scale[pl.ds(b, 1), :]
            pieces = [
                jnp.where(group_index == cand(b, s), row, 0.0).astype(BF16)
                for s in range(slots)
            ]
            left = jnp.concatenate(pieces, axis=1)
            right = jnp.concatenate([kt[b * slots + s] for s in range(slots)], axis=1)
            return total + lax.dot_general(
                right, left, (((1,), (1,)), ((), ())), preferred_element_type=F32
            )

        total = lax.fori_loop(0, blocks, add, jnp.zeros((group_size, groups), F32), unroll=blocks)
        padded = jnp.concatenate([total, jnp.zeros((group_size, 128 - groups), F32)], axis=1)
        return padded.T[:groups]

    send_rows(0, row_scale[...])

    own_load.wait()
    place_copy.wait()
    odd = lax.rem(d, 2) == 1

    def own_share(g, carry):
        raw = own_raw[g].astype(F32)
        raw = jnp.where(odd, raw[8:], raw[:8])
        mean = jnp.sum(raw * raw, axis=-1, keepdims=True) / width
        inv = lax.rsqrt(mean + epsilon) / math.sqrt(width)
        rounded = (raw * inv).astype(BF16).astype(F32)
        own_prior[g] = prior_weight * rounded
        own_rms[g] = jnp.broadcast_to(jnp.sqrt(mean), (8, 128))
        return carry

    lax.fori_loop(0, groups, own_share, 0)
    finish_rows(0)

    def sweep(n, carry):
        send_cols(n, col_sums())
        finish_cols(n)
        send_rows(n + 1, row_sums())

        @pl.when(n == PASSES - 1)
        def turn():
            padded = jnp.concatenate(
                [column[...], jnp.zeros((128 - groups, group_size), F32)], axis=0
            )
            col_turned[...] = padded.T
            mine = col_turned[pl.ds(pl.multiple_of(d * 8, 8), 8), :]
            for g in range(groups):
                own_col[g] = jnp.broadcast_to(mine[:, g : g + 1], (8, 128))

        finish_rows(n + 1)
        return carry

    lax.fori_loop(0, PASSES, sweep, 0)

    at_x = [y * SIDE + lax.rem(x + j, SIDE) for j in range(SIDE)]
    at_y = [lax.rem(y + j, SIDE) * SIDE + x for j in range(SIDE)]
    rounds = groups // 4

    def copy_to(doc, src, dst, send_sem, recv_sem):
        pltpu.make_async_remote_copy(
            src_ref=src,
            dst_ref=dst,
            send_sem=send_sem,
            recv_sem=recv_sem,
            device_id=(doc, c),
            device_id_type=MESH,
        ).start()

    def ring(q, second):
        along_x = (q == 0) != second
        places, pos = (at_x, x) if along_x else (at_y, y)
        return places, [lax.rem(pos + j, SIDE) for j in range(SIDE)]

    def weigh(p, q):
        pieces = []
        for gg in range(2):
            pieces.append(
                jnp.concatenate(
                    [
                        (kt[place(b, 2 * p + gg)].astype(F32) * row_scale[b : b + 1, :]).astype(
                            BF16
                        )
                        for b in range(blocks)
                    ],
                    axis=1,
                )
            )
        left = jnp.concatenate(pieces, axis=0)
        total = jnp.dot(left, docs[...], preferred_element_type=F32)
        for dest in range(n_doc):
            dy, dx = dest // SIDE, dest % SIDE
            first, then = (dx, dy) if q == 0 else (dy, dx)
            rows = jnp.concatenate(
                [
                    total[gg * group_size + 8 * dest : gg * group_size + 8 * dest + 8]
                    for gg in range(2)
                ],
                axis=0,
            ).astype(BF16)
            parts[p, first, 0, then] = rows[:, :half]
            parts[p, first, 1, then] = rows[:, half:]

    def first_far(p, q):
        (_, right, _, left), (_, near, far, back) = ring(q, False)
        copy_to(right, parts.at[p, far, 0], far_recv.at[p, 0], sent_sems.at[p], far_sems.at[p])
        copy_to(left, parts.at[p, far, 1], far_recv.at[p, 1], sent_sems.at[p], far_sems.at[p])

    def first_near(p, q):
        (_, right, _, left), (_, near, far, back) = ring(q, False)
        to = near_recv.at[p]
        copy_to(right, parts.at[p, near, 1], to.at[0, 1], sent_sems.at[p], near_sems.at[p])
        copy_to(left, parts.at[p, back, 0], to.at[1, 0], sent_sems.at[p], near_sems.at[p])

    def first_relay(p, q):
        (_, right, _, left), (_, near, far, back) = ring(q, False)
        whole = far_recv.at[p]
        pltpu.make_async_copy(whole, whole, far_sems.at[p]).wait()
        for h, place, device in ((0, near, right), (1, back, left)):
            parts[p, place, h] = (
                parts[p, place, h].astype(F32) + far_recv[p, h].astype(F32)
            ).astype(BF16)
            copy_to(
                device, parts.at[p, place, h], near_recv.at[p, h, h], sent_sems.at[p], near_sems.at[p]
            )

    def first_end(p, q):
        pos = ring(q, False)[1][0]
        whole = near_recv.at[p]
        pltpu.make_async_copy(whole, whole, near_sems.at[p]).wait()
        for h in range(2):
            total = (
                parts[p, pos, h].astype(F32)
                + near_recv[p, 0, h].astype(F32)
                + near_recv[p, 1, h].astype(F32)
            ).astype(BF16)
            for place in range(SIDE):
                halfway[p, place, h] = total[place]

    def second_start(p, q):
        places, at = ring(q, True)
        for j in (2, 1, 3):
            copy_to(
                places[j], halfway.at[p, at[j]], last_recv.at[p, j - 1], sent2_sems.at[p], last_sems.at[p]
            )

    def second_end(p, q):
        pos = ring(q, True)[1][0]
        whole = last_recv.at[p]
        pltpu.make_async_copy(whole, whole, last_sems.at[p]).wait()
        return [
            halfway[p, pos, h].astype(F32)
            + last_recv[p, 0, h].astype(F32)
            + last_recv[p, 1, h].astype(F32)
            + last_recv[p, 2, h].astype(F32)
            for h in range(2)
        ]

    def finish(p, sums):
        for gg in range(2):
            g = 2 * p + gg
            weight = own_col[g][:, :1]
            prior = own_prior[g]
            low = sums[0][8 * gg : 8 * gg + 8] * weight + prior[:, :half]
            high = sums[1][8 * gg : 8 * gg + 8] * weight + prior[:, half:]
            square = jnp.sum(low * low, axis=-1, keepdims=True) + jnp.sum(
                high * high, axis=-1, keepdims=True
            )
            rescale = own_rms[g][:, :1] * lax.rsqrt(square / width + epsilon)
            out_ref[g, :, :half] = (low * rescale).astype(BF16)
            out_ref[g, :, half:] = (high * rescale).astype(BF16)

    pairs = 2 * rounds

    def turn_of(t, q):
        def begin(p, q):
            weigh(p, q)
            first_far(p, q)

        def middle(p, q):
            first_end(p, q)
            second_start(p, q)

        stages = (
            begin,
            first_relay,
            first_near,
            middle,
            lambda p, q: finish(p, second_end(p, q)),
        )
        for n in ORDER:
            lag, step = LAGS[n], stages[n]
            p = t - lag

            @pl.when((p >= 0) & (p < pairs))
            def _(p=p, lag=lag, step=step):
                step(p, (q - lag) % 2)

    def two_turns(u, carry):
        for q in range(2):
            turn_of(2 * u + q, q)
        return carry

    lax.fori_loop(0, (pairs + LAGS[-1] + 1) // 2, two_turns, 0)

    def sent(p, carry):
        whole = parts.at[p, pl.ds(0, 3)]
        pltpu.make_async_copy(whole, whole, sent_sems.at[p]).wait()
        whole = last_recv.at[p]
        pltpu.make_async_copy(whole, whole, sent2_sems.at[p]).wait()
        return carry

    lax.fori_loop(0, 2 * rounds, sent, 0)
    for n in range(PASSES + 1):
        whole = row_recv.at[n]
        pltpu.make_async_copy(whole, whole, row_send_sems.at[n]).wait()
    for n in range(PASSES):
        whole = col_recv.at[n]
        pltpu.make_async_copy(whole, whole, col_send_sems.at[n]).wait()


def body(n_doc, n_cent, documents, centroids, candidates, counts):
    rows_dev, width = documents.shape
    groups, group_size, unused_width = centroids.shape
    blocks, slots = candidates.shape
    half = width // 2
    pairs = groups // 2
    target = rows_dev * n_doc / (groups * group_size * n_cent)
    names = candidates.T
    live = counts.T
    dma = pltpu.SemaphoreType.DMA
    return pl.pallas_call(
        functools.partial(kernel, n_doc, n_cent, target),
        out_shape=jax.ShapeDtypeStruct((groups, group_size // n_doc, width), BF16),
        in_specs=[pl.BlockSpec(memory_space=pltpu.SMEM)] * 2
        + [pl.BlockSpec(memory_space=pltpu.VMEM)] * 2
        + [pl.BlockSpec(memory_space=pl.ANY)] * 2,
        out_specs=pl.BlockSpec(memory_space=pltpu.VMEM),
        scratch_shapes=[
            pltpu.VMEM((rows_dev, width), BF16),
            pltpu.VMEM((groups, group_size, width), BF16),
            pltpu.VMEM((groups, 16, width), BF16),
            pltpu.VMEM((groups, 8, width), F32),
            pltpu.VMEM((groups, 8, 128), F32),
            pltpu.VMEM((groups, 8, 128), F32),
            pltpu.VMEM((128, 128), F32),
            pltpu.VMEM((blocks * slots + 1, group_size, BLOCK), BF16),
            pltpu.VMEM((blocks, BLOCK), F32),
            pltpu.VMEM((groups, group_size), F32),
            pltpu.VMEM((PASSES + 1, blocks, BLOCK), BF16),
            pltpu.VMEM((PASSES + 1, n_cent - 1, blocks, BLOCK), BF16),
            pltpu.VMEM((PASSES, groups, group_size), BF16),
            pltpu.VMEM((PASSES, n_doc - 1, groups, group_size), BF16),
            pltpu.VMEM((pairs, SIDE, 2, SIDE, 16, half), BF16),
            pltpu.VMEM((pairs, 2, SIDE, 16, half), BF16),
            pltpu.VMEM((pairs, 2, 2, SIDE, 16, half), BF16),
            pltpu.VMEM((pairs, SIDE, 2, 16, half), BF16),
            pltpu.VMEM((pairs, SIDE - 1, 2, 16, half), BF16),
            pltpu.VMEM((groups, 128), jnp.int32),
            pltpu.SMEM((groups, 128), jnp.int32),
            dma((14,)),
            dma((PASSES + 1,)),
            dma((PASSES + 1,)),
            dma((PASSES,)),
            dma((PASSES,)),
            dma((pairs,)),
            dma((pairs,)),
            dma((pairs,)),
            dma((pairs,)),
            dma((pairs,)),
        ],
        compiler_params=pltpu.CompilerParams(
            collective_id=0, has_side_effects=True, vmem_limit_bytes=52 * 1024 * 1024
        ),
    )(names, live, names, live, documents, centroids)


def solution(mesh):
    n_doc, n_cent = mesh.shape["doc"], mesh.shape["cent"]
    return jax.shard_map(
        functools.partial(body, n_doc, n_cent),
        mesh=mesh,
        in_specs=(P("doc", None), P("cent", None, None), P("doc", "cent"), P("doc", "cent")),
        out_specs=P("cent", "doc", None),
        check_vma=False,
    )
```

```python
import functools
import math

import jax
import jax.numpy as jnp
from jax import lax
from jax.experimental import pallas as pl
from jax.experimental.pallas import tpu as pltpu
from jax.sharding import PartitionSpec as P

BLOCK = 128
PASSES = 3
SIDE = 4
ORDER = (0, 1, 2, 3, 4)
LAGS = (0, 3, 7, 10, 14)
DIRECT = (16, 11)
UNROLL = (16, 8, 8)

sharpness = 40.0
smoothing = 0.02
prior_weight = 0.05
epsilon = 1e-06

F32 = jnp.float32
BF16 = jnp.bfloat16
MESH = pl.DeviceIdType.MESH


def kernel(
    n_doc,
    n_cent,
    target,
    names_hbm,
    live_hbm,
    docs_hbm,
    cents_hbm,
    out_ref,
    docs,
    cents,
    own_raw,
    own_prior,
    own_rms,
    own_col,
    col_turned,
    kt,
    row_scale,
    column,
    row_send,
    row_recv,
    col_send,
    col_recv,
    parts,
    far_recv,
    near_recv,
    halfway,
    far_recv2,
    near_recv2,
    names_ref,
    live_ref,
    names_rows,
    live_rows,
    place_rows,
    place_ref,
    load_sems,
    row_send_sems,
    row_recv_sems,
    col_send_sems,
    col_recv_sems,
    far_sems,
    near_sems,
    far2_sems,
    near2_sems,
    sent_sems,
    sent2_sems,
):
    groups, group_size, width = cents.shape
    slots, blocks = names_ref.shape

    def cand(b, s):
        return names_ref[s, b]

    def count(b):
        return live_ref[0, b]

    def place(b, g):
        return place_ref[g, b]

    half = width // 2
    d = lax.axis_index("doc")
    c = lax.axis_index("cent")
    x = lax.rem(d, SIDE)
    y = lax.div(d, SIDE)

    doc_step = docs.shape[0] // 4
    cent_step = groups // 8
    doc_loads = [
        pltpu.make_async_copy(
            docs_hbm.at[pl.ds(n * doc_step, doc_step)],
            docs.at[pl.ds(n * doc_step, doc_step)],
            load_sems.at[n],
        )
        for n in range(4)
    ]
    cent_loads = [
        pltpu.make_async_copy(
            cents_hbm.at[pl.ds(n * cent_step, cent_step)],
            cents.at[pl.ds(n * cent_step, cent_step)],
            load_sems.at[4 + n],
        )
        for n in range(8)
    ]
    own_pair = lax.div(d, 2)
    own_load = pltpu.make_async_copy(
        cents_hbm.at[:, pl.ds(pl.multiple_of(own_pair * 16, 16), 16)], own_raw, load_sems.at[12]
    )
    small_loads = [
        pltpu.make_async_copy(src, dst, load_sems.at[14 + n])
        for n, (src, dst) in enumerate(
            (
                (names_hbm, names_rows),
                (live_hbm, live_rows),
                (names_hbm, names_ref),
                (live_hbm, live_ref),
            )
        )
    ]
    for copy in small_loads + cent_loads + doc_loads + [own_load]:
        copy.start()

    barrier = pltpu.get_barrier_semaphore()
    for j in range(1, n_doc):
        pl.semaphore_signal(
            barrier, inc=1, device_id=(lax.rem(d + j, n_doc), c), device_id_type=MESH
        )
    for j in range(1, n_cent):
        pl.semaphore_signal(
            barrier, inc=1, device_id=(d, lax.rem(c + j, n_cent)), device_id_type=MESH
        )

    def unit(values):
        values = values.astype(F32)
        inv = lax.rsqrt(jnp.sum(values * values, axis=-1, keepdims=True) / width + epsilon)
        return values * (inv / math.sqrt(width))

    def unit_cents(n, carry):
        at = pl.ds(n * cent_step, cent_step)
        cents[at] = unit(cents[at]).astype(BF16)
        return carry

    for n in range(8):
        cent_loads[n].wait()
        lax.fori_loop(n, n + 1, unit_cents, 0)
    for copy in small_loads:
        copy.wait()

    zero_tile = blocks * slots
    group_index = lax.broadcasted_iota(jnp.int32, (groups, blocks), 0)
    block_index = lax.broadcasted_iota(jnp.int32, (groups, blocks), 1)
    tiles = jnp.full((groups, blocks), zero_tile, jnp.int32)
    for s in range(slots):
        named = (names_rows[s : s + 1, :] == group_index) & (live_rows[...] > s)
        tiles = jnp.where(named, block_index * slots + s, tiles)
    place_rows[:, :blocks] = tiles
    place_copy = pltpu.make_async_copy(place_rows, place_ref, load_sems.at[13])
    place_copy.start()

    for n in range(4):
        doc_loads[n].wait()

    scale = sharpness * math.log2(math.e)

    def score(b, carry):
        at = pl.ds(pl.multiple_of(b * BLOCK, BLOCK), BLOCK)
        rows = unit(docs[at, :]).astype(BF16)
        docs[at, :] = rows
        picked = jnp.concatenate([cents[cand(b, s)] for s in range(slots)], axis=0)
        cosine = lax.dot_general(
            picked, rows, (((1,), (1,)), ((), ())), preferred_element_type=F32
        )
        total = jnp.zeros((8, BLOCK), F32)
        for s in range(slots):
            shift = jnp.where(s < count(b), F32(-scale), F32(-1e30))
            tile = jnp.exp2(cosine[s * group_size : (s + 1) * group_size] * scale + shift)
            total = total + jnp.sum(tile.reshape(group_size // 8, 8, BLOCK), axis=0)
            kt[b * slots + s] = tile.astype(BF16)
        row_scale[pl.ds(b, 1), :] = jnp.sum(total, axis=0, keepdims=True)
        return carry

    lax.fori_loop(0, blocks, score, 0, unroll=min(blocks, UNROLL[0]))
    kt[blocks * slots] = jnp.zeros((group_size, BLOCK), BF16)

    pl.semaphore_wait(barrier, n_doc - 1 + n_cent - 1)

    def send_rows(n, value):
        row_send[n] = value.astype(row_send.dtype)
        for j in sorted(range(1, n_cent), key=lambda j: -min(j // 2, n_cent // 2 - j // 2)):
            pltpu.make_async_remote_copy(
                src_ref=row_send.at[n],
                dst_ref=row_recv.at[n, j - 1],
                send_sem=row_send_sems.at[n],
                recv_sem=row_recv_sems.at[n],
                device_id=(d, lax.rem(c + j, n_cent)),
                device_id_type=MESH,
            ).start()

    def finish_rows(n):
        whole = row_recv.at[n]
        pltpu.make_async_copy(whole, whole, row_recv_sems.at[n]).wait()
        total = row_send[n].astype(F32)
        for j in range(n_cent - 1):
            total = total + row_recv[n, j].astype(F32)
        row_scale[...] = 1.0 / total

    def send_cols(n, value):
        col_send[n] = value.astype(col_send.dtype)
        for j in sorted(range(1, n_doc), key=lambda j: -(2 - abs(2 - j % 4) + 2 - abs(2 - j // 4))):
            pltpu.make_async_remote_copy(
                src_ref=col_send.at[n],
                dst_ref=col_recv.at[n, j - 1],
                send_sem=col_send_sems.at[n],
                recv_sem=col_recv_sems.at[n],
                device_id=(lax.rem(d + j, n_doc), c),
                device_id_type=MESH,
            ).start()

    def finish_cols(n):
        whole = col_recv.at[n]
        pltpu.make_async_copy(whole, whole, col_recv_sems.at[n]).wait()
        total = col_send[n].astype(F32)
        for j in range(n_doc - 1):
            total = total + col_recv[n, j].astype(F32)
        column[...] = target / (total + smoothing)

    def row_sums():
        row_index = lax.broadcasted_iota(jnp.int32, (blocks, BLOCK), 0)

        def add(b, total):
            pieces = [
                jnp.where(row_index == b, column[pl.ds(cand(b, s), 1), :], 0.0).astype(BF16)
                for s in range(slots)
            ]
            left = jnp.concatenate(pieces, axis=1)
            right = jnp.concatenate([kt[b * slots + s] for s in range(slots)], axis=0)
            return total + jnp.dot(left, right, preferred_element_type=F32)

        return lax.fori_loop(0, blocks, add, jnp.zeros((blocks, BLOCK), F32), unroll=min(blocks, UNROLL[1]))

    def col_sums():
        group_index = lax.broadcasted_iota(jnp.int32, (groups, BLOCK), 0)

        def add(b, total):
            row = row_scale[pl.ds(b, 1), :]
            pieces = [
                jnp.where(group_index == cand(b, s), row, 0.0).astype(BF16)
                for s in range(slots)
            ]
            left = jnp.concatenate(pieces, axis=1)
            right = jnp.concatenate([kt[b * slots + s] for s in range(slots)], axis=1)
            return total + lax.dot_general(
                right, left, (((1,), (1,)), ((), ())), preferred_element_type=F32
            )

        total = lax.fori_loop(0, blocks, add, jnp.zeros((group_size, groups), F32), unroll=min(blocks, UNROLL[2]))
        padded = jnp.concatenate([total, jnp.zeros((group_size, 128 - groups), F32)], axis=1)
        return padded.T[:groups]

    send_rows(0, row_scale[...])

    own_load.wait()
    place_copy.wait()
    odd = lax.rem(d, 2) == 1

    def own_share(g, carry):
        raw = own_raw[g].astype(F32)
        raw = jnp.where(odd, raw[8:], raw[:8])
        mean = jnp.sum(raw * raw, axis=-1, keepdims=True) / width
        inv = lax.rsqrt(mean + epsilon) / math.sqrt(width)
        rounded = (raw * inv).astype(BF16).astype(F32)
        own_prior[g] = prior_weight * rounded
        own_rms[g] = jnp.broadcast_to(jnp.sqrt(mean), (8, 128))
        return carry

    lax.fori_loop(0, groups, own_share, 0)
    finish_rows(0)

    def sweep(n, carry):
        send_cols(n, col_sums())
        finish_cols(n)
        send_rows(n + 1, row_sums())

        @pl.when(n == PASSES - 1)
        def turn():
            padded = jnp.concatenate(
                [column[...], jnp.zeros((128 - groups, group_size), F32)], axis=0
            )
            col_turned[...] = padded.T
            mine = col_turned[pl.ds(pl.multiple_of(d * 8, 8), 8), :]
            for g in range(groups):
                own_col[g] = jnp.broadcast_to(mine[:, g : g + 1], (8, 128))

        finish_rows(n + 1)
        return carry

    lax.fori_loop(0, PASSES, sweep, 0)

    at_x = [y * SIDE + lax.rem(x + j, SIDE) for j in range(SIDE)]
    at_y = [lax.rem(y + j, SIDE) * SIDE + x for j in range(SIDE)]
    rounds = groups // 4

    def copy_to(doc, src, dst, send_sem, recv_sem):
        pltpu.make_async_remote_copy(
            src_ref=src,
            dst_ref=dst,
            send_sem=send_sem,
            recv_sem=recv_sem,
            device_id=(doc, c),
            device_id_type=MESH,
        ).start()

    def ring(q, second):
        along_x = (q == 0) != second
        places, pos = (at_x, x) if along_x else (at_y, y)
        right, left = places[1], places[3]
        return (
            right,
            places[2],
            left,
            pos,
            lax.rem(pos + 1, SIDE),
            lax.rem(pos + 2, SIDE),
            lax.rem(pos + 3, SIDE),
        )

    def weigh(p, q):
        pieces = []
        for gg in range(2):
            pieces.append(
                jnp.concatenate(
                    [
                        (kt[place(b, 2 * p + gg)].astype(F32) * row_scale[b : b + 1, :]).astype(
                            BF16
                        )
                        for b in range(blocks)
                    ],
                    axis=1,
                )
            )
        left = jnp.concatenate(pieces, axis=0)
        total = jnp.dot(left, docs[...], preferred_element_type=F32)
        for dest in range(n_doc):
            dy, dx = dest // SIDE, dest % SIDE
            first, then = (dx, dy) if q == 0 else (dy, dx)
            rows = jnp.concatenate(
                [
                    total[gg * group_size + 8 * dest : gg * group_size + 8 * dest + 8]
                    for gg in range(2)
                ],
                axis=0,
            ).astype(BF16)
            parts[p, first, 0, then] = rows[:, :half]
            parts[p, first, 1, then] = rows[:, half:]

    def leg_start(p, q, second):
        right, across, left, pos, near, far, back = ring(q, second)
        if second:
            piece = lambda place, h: halfway.at[p, h, place]
            far_to, near_to = far_recv2, near_recv2
            far_sem, near_sem, sent = far2_sems.at[p], near2_sems.at[p], sent2_sems.at[p]
        else:
            piece = lambda place, h: parts.at[p, place, h]
            far_to, near_to = far_recv, near_recv
            far_sem, near_sem, sent = far_sems.at[p], near_sems.at[p], sent_sems.at[p]
        @pl.when(p < DIRECT[second])
        def _():
            copy_to(right, piece(far, 0), far_to.at[p, 0], sent, far_sem)
            copy_to(left, piece(far, 1), far_to.at[p, 1], sent, far_sem)

        @pl.when(p >= DIRECT[second])
        def _():
            for h in range(2):
                copy_to(across, piece(far, h), far_to.at[p, h], sent, far_sem)
            copy_to(right, piece(near, 0), near_to.at[p, 0, 0], sent, near_sem)
            copy_to(left, piece(back, 1), near_to.at[p, 1, 1], sent, near_sem)

        copy_to(right, piece(near, 1), near_to.at[p, 0, 1], sent, near_sem)
        copy_to(left, piece(back, 0), near_to.at[p, 1, 0], sent, near_sem)

    def leg_relay(p, q, second):
        right, across, left, pos, near, far, back = ring(q, second)
        if second:
            got, near_to = far_recv2, near_recv2
            far_sem, near_sem, sent = far2_sems.at[p], near2_sems.at[p], sent2_sems.at[p]
        else:
            got, near_to = far_recv, near_recv
            far_sem, near_sem, sent = far_sems.at[p], near_sems.at[p], sent_sems.at[p]
        whole = got.at[p]
        pltpu.make_async_copy(whole, whole, far_sem).wait()
        for h, place, device in ((0, near, right), (1, back, left)):
            if second:
                halfway[p, h, place] = (
                    halfway[p, h, place].astype(F32) + got[p, h].astype(F32)
                ).astype(BF16)
                src = halfway.at[p, h, place]
            else:
                parts[p, place, h] = (
                    parts[p, place, h].astype(F32) + got[p, h].astype(F32)
                ).astype(BF16)
                src = parts.at[p, place, h]
            copy_to(device, src, near_to.at[p, h, h], sent, near_sem)

    def leg_end(p, q, second):
        pos = ring(q, second)[3]
        got = near_recv2 if second else near_recv
        far_got, far_sem = (far_recv2, far2_sems) if second else (far_recv, far_sems)
        near_sem = near2_sems if second else near_sems
        whole = got.at[p]
        pltpu.make_async_copy(whole, whole, near_sem.at[p]).wait()

        @pl.when(p >= DIRECT[second])
        def _():
            whole = far_got.at[p]
            pltpu.make_async_copy(whole, whole, far_sem.at[p]).wait()
            for h in range(2):
                got[p, 0, h] = (got[p, 0, h].astype(F32) + far_got[p, h].astype(F32)).astype(BF16)

        if second:
            return [
                halfway[p, h, pos].astype(F32)
                + near_recv2[p, 0, h].astype(F32)
                + near_recv2[p, 1, h].astype(F32)
                for h in range(2)
            ]
        for h in range(2):
            halfway[p, h] = (
                parts[p, pos, h].astype(F32)
                + near_recv[p, 0, h].astype(F32)
                + near_recv[p, 1, h].astype(F32)
            ).astype(BF16)

    def finish(p, sums):
        for gg in range(2):
            g = 2 * p + gg
            weight = own_col[g][:, :1]
            prior = own_prior[g]
            low = sums[0][8 * gg : 8 * gg + 8] * weight + prior[:, :half]
            high = sums[1][8 * gg : 8 * gg + 8] * weight + prior[:, half:]
            square = jnp.sum(low * low, axis=-1, keepdims=True) + jnp.sum(
                high * high, axis=-1, keepdims=True
            )
            rescale = own_rms[g][:, :1] * lax.rsqrt(square / width + epsilon)
            out_ref[g, :, :half] = (low * rescale).astype(BF16)
            out_ref[g, :, half:] = (high * rescale).astype(BF16)

    pairs = 2 * rounds

    def turn_of(t, q):
        def begin(p, q):
            weigh(p, q)
            leg_start(p, q, False)

        def relay_if(p, q, second):
            @pl.when(p < DIRECT[second])
            def _():
                leg_relay(p, q, second)

        def middle(p, q):
            leg_end(p, q, False)
            leg_start(p, q, True)

        stages = (
            begin,
            lambda p, q: relay_if(p, q, False),
            middle,
            lambda p, q: relay_if(p, q, True),
            lambda p, q: finish(p, leg_end(p, q, True)),
        )
        for n in ORDER:
            lag, step = LAGS[n], stages[n]
            p = t - lag

            @pl.when((p >= 0) & (p < pairs))
            def _(p=p, lag=lag, step=step):
                step(p, (q - lag) % 2)

    def two_turns(u, carry):
        for q in range(2):
            turn_of(2 * u + q, q)
        return carry

    lax.fori_loop(0, (pairs + LAGS[-1] + 1) // 2, two_turns, 0)

    def sent(p, carry):
        whole = parts.at[p, pl.ds(0, 3)]
        pltpu.make_async_copy(whole, whole, sent_sems.at[p]).wait()
        whole = halfway.at[p, :, pl.ds(0, 3)]
        pltpu.make_async_copy(whole, whole, sent2_sems.at[p]).wait()
        return carry

    lax.fori_loop(0, 2 * rounds, sent, 0)
    for n in range(PASSES + 1):
        whole = row_recv.at[n]
        pltpu.make_async_copy(whole, whole, row_send_sems.at[n]).wait()
    for n in range(PASSES):
        whole = col_recv.at[n]
        pltpu.make_async_copy(whole, whole, col_send_sems.at[n]).wait()


def body(n_doc, n_cent, documents, centroids, candidates, counts):
    rows_dev, width = documents.shape
    groups, group_size, unused_width = centroids.shape
    blocks, slots = candidates.shape
    half = width // 2
    pairs = groups // 2
    target = rows_dev * n_doc / (groups * group_size * n_cent)
    names = candidates.T
    live = counts.T
    dma = pltpu.SemaphoreType.DMA
    return pl.pallas_call(
        functools.partial(kernel, n_doc, n_cent, target),
        out_shape=jax.ShapeDtypeStruct((groups, group_size // n_doc, width), BF16),
        in_specs=[pl.BlockSpec(memory_space=pltpu.HBM)] * 4,
        out_specs=pl.BlockSpec(memory_space=pltpu.VMEM),
        scratch_shapes=[
            pltpu.VMEM((rows_dev, width), BF16),
            pltpu.VMEM((groups, group_size, width), BF16),
            pltpu.VMEM((groups, 16, width), BF16),
            pltpu.VMEM((groups, 8, width), F32),
            pltpu.VMEM((groups, 8, 128), F32),
            pltpu.VMEM((groups, 8, 128), F32),
            pltpu.VMEM((128, 128), F32),
            pltpu.VMEM((blocks * slots + 1, group_size, BLOCK), BF16),
            pltpu.VMEM((blocks, BLOCK), F32),
            pltpu.VMEM((groups, group_size), F32),
            pltpu.VMEM((PASSES + 1, blocks, BLOCK), BF16),
            pltpu.VMEM((PASSES + 1, n_cent - 1, blocks, BLOCK), BF16),
            pltpu.VMEM((PASSES, groups, group_size), BF16),
            pltpu.VMEM((PASSES, n_doc - 1, groups, group_size), BF16),
            pltpu.VMEM((pairs, SIDE, 2, SIDE, 16, half), BF16),
            pltpu.VMEM((pairs, 2, SIDE, 16, half), BF16),
            pltpu.VMEM((pairs, 2, 2, SIDE, 16, half), BF16),
            pltpu.VMEM((pairs, 2, SIDE, 16, half), BF16),
            pltpu.VMEM((pairs, 2, 16, half), BF16),
            pltpu.VMEM((pairs, 2, 2, 16, half), BF16),
            pltpu.SMEM((slots, blocks), jnp.int32),
            pltpu.SMEM((1, blocks), jnp.int32),
            pltpu.VMEM((slots, blocks), jnp.int32),
            pltpu.VMEM((1, blocks), jnp.int32),
            pltpu.VMEM((groups, 128), jnp.int32),
            pltpu.SMEM((groups, 128), jnp.int32),
            dma((18,)),
            dma((PASSES + 1,)),
            dma((PASSES + 1,)),
            dma((PASSES,)),
            dma((PASSES,)),
            dma((pairs,)),
            dma((pairs,)),
            dma((pairs,)),
            dma((pairs,)),
            dma((pairs,)),
            dma((pairs,)),
        ],
        compiler_params=pltpu.CompilerParams(
            collective_id=0, has_side_effects=True, vmem_limit_bytes=52 * 1024 * 1024
        ),
    )(names, live, documents, centroids)


def solution(mesh):
    n_doc, n_cent = mesh.shape["doc"], mesh.shape["cent"]
    return jax.shard_map(
        functools.partial(body, n_doc, n_cent),
        mesh=mesh,
        in_specs=(P("doc", None), P("cent", None, None), P("doc", "cent"), P("doc", "cent")),
        out_specs=P("cent", "doc", None),
        check_vma=False,
    )
```

```python
import functools
import math

import jax
import jax.numpy as jnp
from jax import lax
from jax.experimental import pallas as pl
from jax.experimental.pallas import tpu as pltpu
from jax.sharding import PartitionSpec as P

BLOCK = 128
PASSES = 3
SIDE = 4
ORDER = (0, 1, 2, 3, 4)
LAGS = (0, 3, 6, 9, 12)
DIRECT = (16, 11)
UNROLL = (16, 8, 8)

sharpness = 40.0
smoothing = 0.02
prior_weight = 0.05
epsilon = 1e-06

F32 = jnp.float32
BF16 = jnp.bfloat16
MESH = pl.DeviceIdType.MESH


def kernel(
    n_doc,
    n_cent,
    target,
    lists_hbm,
    docs_hbm,
    cents_hbm,
    out_ref,
    docs,
    cents,
    own_raw,
    own_prior,
    own_rms,
    own_col,
    col_turned,
    kt,
    row_scale,
    column,
    row_send,
    row_recv,
    col_send,
    col_recv,
    parts,
    far_recv,
    near_recv,
    halfway,
    far_recv2,
    near_recv2,
    lists_ref,
    lists_rows,
    place_rows,
    place_ref,
    load_sems,
    row_send_sems,
    row_recv_sems,
    col_send_sems,
    col_recv_sems,
    far_sems,
    near_sems,
    far2_sems,
    near2_sems,
    sent_sems,
    sent2_sems,
):
    groups, group_size, width = cents.shape
    slots, blocks = lists_ref.shape[0] - 1, lists_ref.shape[1]

    def cand(b, s):
        return lists_ref[s, b]

    def count(b):
        return lists_ref[slots, b]

    def place(b, g):
        return place_ref[g, b]

    half = width // 2
    d = lax.axis_index("doc")
    c = lax.axis_index("cent")
    x = lax.rem(d, SIDE)
    y = lax.div(d, SIDE)

    doc_step = docs.shape[0] // 4
    cent_step = groups // 8
    doc_loads = [
        pltpu.make_async_copy(
            docs_hbm.at[pl.ds(n * doc_step, doc_step)],
            docs.at[pl.ds(n * doc_step, doc_step)],
            load_sems.at[n],
        )
        for n in range(4)
    ]
    cent_loads = [
        pltpu.make_async_copy(
            cents_hbm.at[pl.ds(n * cent_step, cent_step)],
            cents.at[pl.ds(n * cent_step, cent_step)],
            load_sems.at[4 + n],
        )
        for n in range(8)
    ]
    own_pair = lax.div(d, 2)
    own_load = pltpu.make_async_copy(
        cents_hbm.at[:, pl.ds(pl.multiple_of(own_pair * 16, 16), 16)], own_raw, load_sems.at[12]
    )
    small_loads = [
        pltpu.make_async_copy(src, dst, load_sems.at[14 + n])
        for n, (src, dst) in enumerate(
            ((lists_hbm, lists_rows), (lists_hbm, lists_ref))
        )
    ]
    for copy in small_loads + cent_loads + doc_loads + [own_load]:
        copy.start()

    barrier = pltpu.get_barrier_semaphore()
    for j in range(1, n_doc):
        pl.semaphore_signal(
            barrier, inc=1, device_id=(lax.rem(d + j, n_doc), c), device_id_type=MESH
        )
    for j in range(1, n_cent):
        pl.semaphore_signal(
            barrier, inc=1, device_id=(d, lax.rem(c + j, n_cent)), device_id_type=MESH
        )

    def unit(values):
        values = values.astype(F32)
        inv = lax.rsqrt(jnp.sum(values * values, axis=-1, keepdims=True) / width + epsilon)
        return values * (inv / math.sqrt(width))

    def cent_load(n):
        at = pl.ds(n * cent_step, cent_step)
        return pltpu.make_async_copy(cents_hbm.at[at], cents.at[at], load_sems.at[4 + n])

    def unit_cents(n, carry):
        at = pl.ds(n * cent_step, cent_step)
        cent_load(n).wait()
        cents[at] = unit(cents[at]).astype(BF16)
        return carry

    lax.fori_loop(0, 8, unit_cents, 0)
    for copy in small_loads:
        copy.wait()

    zero_tile = blocks * slots
    group_index = lax.broadcasted_iota(jnp.int32, (groups, blocks), 0)
    block_index = lax.broadcasted_iota(jnp.int32, (groups, blocks), 1)
    tiles = jnp.full((groups, blocks), zero_tile, jnp.int32)
    for s in range(slots):
        named = (lists_rows[s : s + 1, :] == group_index) & (lists_rows[slots:, :] > s)
        tiles = jnp.where(named, block_index * slots + s, tiles)
    place_rows[:, :blocks] = tiles
    place_copy = pltpu.make_async_copy(place_rows, place_ref, load_sems.at[13])
    place_copy.start()

    for n in range(4):
        doc_loads[n].wait()

    scale = sharpness * math.log2(math.e)

    def score(b, carry):
        at = pl.ds(pl.multiple_of(b * BLOCK, BLOCK), BLOCK)
        rows = unit(docs[at, :]).astype(BF16)
        docs[at, :] = rows
        picked = jnp.concatenate([cents[cand(b, s)] for s in range(slots)], axis=0)
        cosine = lax.dot_general(
            picked, rows, (((1,), (1,)), ((), ())), preferred_element_type=F32
        )
        total = jnp.zeros((8, BLOCK), F32)
        for s in range(slots):
            shift = jnp.where(s < count(b), F32(-scale), F32(-1e30))
            tile = jnp.exp2(cosine[s * group_size : (s + 1) * group_size] * scale + shift)
            total = total + jnp.sum(tile.reshape(group_size // 8, 8, BLOCK), axis=0)
            kt[b * slots + s] = tile.astype(BF16)
        row_scale[pl.ds(b, 1), :] = jnp.sum(total, axis=0, keepdims=True)
        return carry

    lax.fori_loop(0, blocks, score, 0, unroll=min(blocks, UNROLL[0]))
    kt[blocks * slots] = jnp.zeros((group_size, BLOCK), BF16)

    pl.semaphore_wait(barrier, n_doc - 1 + n_cent - 1)

    def send_rows(n, value):
        row_send[n] = value.astype(row_send.dtype)
        for j in sorted(range(1, n_cent), key=lambda j: -min(j // 2, n_cent // 2 - j // 2)):
            pltpu.make_async_remote_copy(
                src_ref=row_send.at[n],
                dst_ref=row_recv.at[n, j - 1],
                send_sem=row_send_sems.at[n],
                recv_sem=row_recv_sems.at[n],
                device_id=(d, lax.rem(c + j, n_cent)),
                device_id_type=MESH,
            ).start()

    def finish_rows(n):
        whole = row_recv.at[n]
        pltpu.make_async_copy(whole, whole, row_recv_sems.at[n]).wait()
        total = row_send[n].astype(F32)
        for j in range(n_cent - 1):
            total = total + row_recv[n, j].astype(F32)
        row_scale[...] = 1.0 / total

    def send_cols(n, value):
        col_send[n] = value.astype(col_send.dtype)
        for j in sorted(range(1, n_doc), key=lambda j: -(2 - abs(2 - j % 4) + 2 - abs(2 - j // 4))):
            pltpu.make_async_remote_copy(
                src_ref=col_send.at[n],
                dst_ref=col_recv.at[n, j - 1],
                send_sem=col_send_sems.at[n],
                recv_sem=col_recv_sems.at[n],
                device_id=(lax.rem(d + j, n_doc), c),
                device_id_type=MESH,
            ).start()

    def finish_cols(n):
        whole = col_recv.at[n]
        pltpu.make_async_copy(whole, whole, col_recv_sems.at[n]).wait()
        total = col_send[n].astype(F32)
        for j in range(n_doc - 1):
            total = total + col_recv[n, j].astype(F32)
        column[...] = target / (total + smoothing)

    def row_sums():
        row_index = lax.broadcasted_iota(jnp.int32, (blocks, BLOCK), 0)

        def add(b, total):
            pieces = [
                jnp.where(row_index == b, column[pl.ds(cand(b, s), 1), :], 0.0).astype(BF16)
                for s in range(slots)
            ]
            left = jnp.concatenate(pieces, axis=1)
            right = jnp.concatenate([kt[b * slots + s] for s in range(slots)], axis=0)
            return total + jnp.dot(left, right, preferred_element_type=F32)

        return lax.fori_loop(0, blocks, add, jnp.zeros((blocks, BLOCK), F32), unroll=min(blocks, UNROLL[1]))

    def col_sums():
        group_index = lax.broadcasted_iota(jnp.int32, (groups, BLOCK), 0)

        def add(b, total):
            row = row_scale[pl.ds(b, 1), :]
            pieces = [
                jnp.where(group_index == cand(b, s), row, 0.0).astype(BF16)
                for s in range(slots)
            ]
            left = jnp.concatenate(pieces, axis=1)
            right = jnp.concatenate([kt[b * slots + s] for s in range(slots)], axis=1)
            return total + lax.dot_general(
                right, left, (((1,), (1,)), ((), ())), preferred_element_type=F32
            )

        total = lax.fori_loop(0, blocks, add, jnp.zeros((group_size, groups), F32), unroll=min(blocks, UNROLL[2]))
        padded = jnp.concatenate([total, jnp.zeros((group_size, 128 - groups), F32)], axis=1)
        return padded.T[:groups]

    send_rows(0, row_scale[...])

    own_load.wait()
    place_copy.wait()
    odd = lax.rem(d, 2) == 1

    def own_share(g, carry):
        raw = own_raw[g].astype(F32)
        raw = jnp.where(odd, raw[8:], raw[:8])
        mean = jnp.sum(raw * raw, axis=-1, keepdims=True) / width
        inv = lax.rsqrt(mean + epsilon) / math.sqrt(width)
        rounded = (raw * inv).astype(BF16).astype(F32)
        own_prior[g] = prior_weight * rounded
        own_rms[g] = jnp.broadcast_to(jnp.sqrt(mean), (8, 128))
        return carry

    lax.fori_loop(0, groups, own_share, 0)
    finish_rows(0)

    def sweep(n, carry):
        send_cols(n, col_sums())
        finish_cols(n)
        send_rows(n + 1, row_sums())

        @pl.when(n == PASSES - 1)
        def turn():
            padded = jnp.concatenate(
                [column[...], jnp.zeros((128 - groups, group_size), F32)], axis=0
            )
            col_turned[...] = padded.T
            mine = col_turned[pl.ds(pl.multiple_of(d * 8, 8), 8), :]
            for g in range(groups):
                own_col[g] = jnp.broadcast_to(mine[:, g : g + 1], (8, 128))

        finish_rows(n + 1)
        return carry

    lax.fori_loop(0, PASSES, sweep, 0)

    at_x = [y * SIDE + lax.rem(x + j, SIDE) for j in range(SIDE)]
    at_y = [lax.rem(y + j, SIDE) * SIDE + x for j in range(SIDE)]
    rounds = groups // 4

    def copy_to(doc, src, dst, send_sem, recv_sem):
        pltpu.make_async_remote_copy(
            src_ref=src,
            dst_ref=dst,
            send_sem=send_sem,
            recv_sem=recv_sem,
            device_id=(doc, c),
            device_id_type=MESH,
        ).start()

    def ring(q, second):
        along_x = (q == 0) != second
        places, pos = (at_x, x) if along_x else (at_y, y)
        right, left = places[1], places[3]
        return (
            right,
            places[2],
            left,
            pos,
            lax.rem(pos + 1, SIDE),
            lax.rem(pos + 2, SIDE),
            lax.rem(pos + 3, SIDE),
        )

    def weigh(p, q):
        pieces = []
        for gg in range(2):
            pieces.append(
                jnp.concatenate(
                    [
                        (kt[place(b, 2 * p + gg)].astype(F32) * row_scale[b : b + 1, :]).astype(
                            BF16
                        )
                        for b in range(blocks)
                    ],
                    axis=1,
                )
            )
        left = jnp.concatenate(pieces, axis=0)
        total = jnp.dot(left, docs[...], preferred_element_type=F32)
        for dest in range(n_doc):
            dy, dx = dest // SIDE, dest % SIDE
            first, then = (dx, dy) if q == 0 else (dy, dx)
            rows = jnp.concatenate(
                [
                    total[gg * group_size + 8 * dest : gg * group_size + 8 * dest + 8]
                    for gg in range(2)
                ],
                axis=0,
            ).astype(BF16)
            parts[p, first, 0, then] = rows[:, :half]
            parts[p, first, 1, then] = rows[:, half:]

    def leg_start(p, q, second):
        right, across, left, pos, near, far, back = ring(q, second)
        if second:
            piece = lambda place, h: halfway.at[p, h, place]
            far_to, near_to = far_recv2, near_recv2
            far_sem, near_sem, sent = far2_sems.at[p], near2_sems.at[p], sent2_sems.at[p]
        else:
            piece = lambda place, h: parts.at[p, place, h]
            far_to, near_to = far_recv, near_recv
            far_sem, near_sem, sent = far_sems.at[p], near_sems.at[p], sent_sems.at[p]
        @pl.when(p < DIRECT[second])
        def _():
            copy_to(right, piece(far, 0), far_to.at[p, 0], sent, far_sem)
            copy_to(left, piece(far, 1), far_to.at[p, 1], sent, far_sem)

        @pl.when(p >= DIRECT[second])
        def _():
            for h in range(2):
                copy_to(across, piece(far, h), far_to.at[p, h], sent, far_sem)
            copy_to(right, piece(near, 0), near_to.at[p, 0, 0], sent, near_sem)
            copy_to(left, piece(back, 1), near_to.at[p, 1, 1], sent, near_sem)

        copy_to(right, piece(near, 1), near_to.at[p, 0, 1], sent, near_sem)
        copy_to(left, piece(back, 0), near_to.at[p, 1, 0], sent, near_sem)

    def leg_relay(p, q, second):
        right, across, left, pos, near, far, back = ring(q, second)
        if second:
            got, near_to = far_recv2, near_recv2
            far_sem, near_sem, sent = far2_sems.at[p], near2_sems.at[p], sent2_sems.at[p]
        else:
            got, near_to = far_recv, near_recv
            far_sem, near_sem, sent = far_sems.at[p], near_sems.at[p], sent_sems.at[p]
        whole = got.at[p]
        pltpu.make_async_copy(whole, whole, far_sem).wait()
        for h, place, device in ((0, near, right), (1, back, left)):
            if second:
                halfway[p, h, place] = (
                    halfway[p, h, place].astype(F32) + got[p, h].astype(F32)
                ).astype(BF16)
                src = halfway.at[p, h, place]
            else:
                parts[p, place, h] = (
                    parts[p, place, h].astype(F32) + got[p, h].astype(F32)
                ).astype(BF16)
                src = parts.at[p, place, h]
            copy_to(device, src, near_to.at[p, h, h], sent, near_sem)

    def leg_end(p, q, second):
        pos = ring(q, second)[3]
        got = near_recv2 if second else near_recv
        far_got, far_sem = (far_recv2, far2_sems) if second else (far_recv, far_sems)
        near_sem = near2_sems if second else near_sems
        whole = got.at[p]
        pltpu.make_async_copy(whole, whole, near_sem.at[p]).wait()

        @pl.when(p >= DIRECT[second])
        def _():
            whole = far_got.at[p]
            pltpu.make_async_copy(whole, whole, far_sem.at[p]).wait()
            for h in range(2):
                got[p, 0, h] = (got[p, 0, h].astype(F32) + far_got[p, h].astype(F32)).astype(BF16)

        if second:
            return [
                halfway[p, h, pos].astype(F32)
                + near_recv2[p, 0, h].astype(F32)
                + near_recv2[p, 1, h].astype(F32)
                for h in range(2)
            ]
        for h in range(2):
            halfway[p, h] = (
                parts[p, pos, h].astype(F32)
                + near_recv[p, 0, h].astype(F32)
                + near_recv[p, 1, h].astype(F32)
            ).astype(BF16)

    def finish(p, sums):
        for gg in range(2):
            g = 2 * p + gg
            weight = own_col[g][:, :1]
            prior = own_prior[g]
            low = sums[0][8 * gg : 8 * gg + 8] * weight + prior[:, :half]
            high = sums[1][8 * gg : 8 * gg + 8] * weight + prior[:, half:]
            square = jnp.sum(low * low, axis=-1, keepdims=True) + jnp.sum(
                high * high, axis=-1, keepdims=True
            )
            rescale = own_rms[g][:, :1] * lax.rsqrt(square / width + epsilon)
            out_ref[g, :, :half] = (low * rescale).astype(BF16)
            out_ref[g, :, half:] = (high * rescale).astype(BF16)

    pairs = 2 * rounds

    def turn_of(t, q):
        def begin(p, q):
            weigh(p, q)
            leg_start(p, q, False)

        def relay_if(p, q, second):
            @pl.when(p < DIRECT[second])
            def _():
                leg_relay(p, q, second)

        def middle(p, q):
            leg_end(p, q, False)
            leg_start(p, q, True)

        def last(p, q):
            finish(p, leg_end(p, q, True))
            pair_sent(p)

        stages = (
            begin,
            lambda p, q: relay_if(p, q, False),
            middle,
            lambda p, q: relay_if(p, q, True),
            last,
        )
        for n in ORDER:
            lag, step = LAGS[n], stages[n]
            p = t - lag

            @pl.when((p >= 0) & (p < pairs))
            def _(p=p, lag=lag, step=step):
                step(p, (q - lag) % 2)

    def sums_sent():
        for n in range(PASSES + 1):
            whole = row_recv.at[n]
            pltpu.make_async_copy(whole, whole, row_send_sems.at[n]).wait()
        for n in range(PASSES):
            whole = col_recv.at[n]
            pltpu.make_async_copy(whole, whole, col_send_sems.at[n]).wait()

    def pair_sent(p):
        whole = parts.at[p, pl.ds(0, 3)]
        pltpu.make_async_copy(whole, whole, sent_sems.at[p]).wait()
        whole = halfway.at[p, :, pl.ds(0, 3)]
        pltpu.make_async_copy(whole, whole, sent2_sems.at[p]).wait()

    def two_turns(u, carry):
        pl.when(u == 1)(sums_sent)
        for q in range(2):
            turn_of(2 * u + q, q)
        return carry

    lax.fori_loop(0, (pairs + LAGS[-1] + 1) // 2, two_turns, 0)


def body(n_doc, n_cent, documents, centroids, candidates, counts):
    rows_dev, width = documents.shape
    groups, group_size, unused_width = centroids.shape
    blocks, slots = candidates.shape
    half = width // 2
    pairs = groups // 2
    target = rows_dev * n_doc / (groups * group_size * n_cent)
    lists = jnp.concatenate([candidates.T, counts.T], axis=0)
    dma = pltpu.SemaphoreType.DMA
    return pl.pallas_call(
        functools.partial(kernel, n_doc, n_cent, target),
        out_shape=jax.ShapeDtypeStruct((groups, group_size // n_doc, width), BF16),
        in_specs=[pl.BlockSpec(memory_space=pltpu.HBM)] * 3,
        out_specs=pl.BlockSpec(memory_space=pltpu.VMEM),
        scratch_shapes=[
            pltpu.VMEM((rows_dev, width), BF16),
            pltpu.VMEM((groups, group_size, width), BF16),
            pltpu.VMEM((groups, 16, width), BF16),
            pltpu.VMEM((groups, 8, width), F32),
            pltpu.VMEM((groups, 8, 128), F32),
            pltpu.VMEM((groups, 8, 128), F32),
            pltpu.VMEM((128, 128), F32),
            pltpu.VMEM((blocks * slots + 1, group_size, BLOCK), BF16),
            pltpu.VMEM((blocks, BLOCK), F32),
            pltpu.VMEM((groups, group_size), F32),
            pltpu.VMEM((PASSES + 1, blocks, BLOCK), BF16),
            pltpu.VMEM((PASSES + 1, n_cent - 1, blocks, BLOCK), BF16),
            pltpu.VMEM((PASSES, groups, group_size), BF16),
            pltpu.VMEM((PASSES, n_doc - 1, groups, group_size), BF16),
            pltpu.VMEM((pairs, SIDE, 2, SIDE, 16, half), BF16),
            pltpu.VMEM((pairs, 2, SIDE, 16, half), BF16),
            pltpu.VMEM((pairs, 2, 2, SIDE, 16, half), BF16),
            pltpu.VMEM((pairs, 2, SIDE, 16, half), BF16),
            pltpu.VMEM((pairs, 2, 16, half), BF16),
            pltpu.VMEM((pairs, 2, 2, 16, half), BF16),
            pltpu.SMEM((slots + 1, blocks), jnp.int32),
            pltpu.VMEM((slots + 1, blocks), jnp.int32),
            pltpu.VMEM((groups, 128), jnp.int32),
            pltpu.SMEM((groups, 128), jnp.int32),
            dma((18,)),
            dma((PASSES + 1,)),
            dma((PASSES + 1,)),
            dma((PASSES,)),
            dma((PASSES,)),
            dma((pairs,)),
            dma((pairs,)),
            dma((pairs,)),
            dma((pairs,)),
            dma((pairs,)),
            dma((pairs,)),
        ],
        compiler_params=pltpu.CompilerParams(
            collective_id=0, has_side_effects=True, vmem_limit_bytes=52 * 1024 * 1024
        ),
    )(lists, documents, centroids)


def solution(mesh):
    n_doc, n_cent = mesh.shape["doc"], mesh.shape["cent"]
    return jax.shard_map(
        functools.partial(body, n_doc, n_cent),
        mesh=mesh,
        in_specs=(P("doc", None), P("cent", None, None), P("doc", "cent"), P("doc", "cent")),
        out_specs=P("cent", "doc", None),
        check_vma=False,
    )
```

```python
import functools
import math

import jax
import jax.numpy as jnp
from jax import lax
from jax.experimental import pallas as pl
from jax.experimental.pallas import tpu as pltpu
from jax.sharding import PartitionSpec as P

BLOCK = 128
PASSES = 3
SIDE = 4
ORDER = (0, 1, 2, 3, 4)
LAGS = (0, 3, 6, 9, 12)
DIRECT = (16, 11)
UNROLL = (16, 8, 8)

sharpness = 40.0
smoothing = 0.02
prior_weight = 0.05
epsilon = 1e-06

F32 = jnp.float32
BF16 = jnp.bfloat16
MESH = pl.DeviceIdType.MESH


def kernel(
    n_doc,
    n_cent,
    target,
    lists_hbm,
    docs_hbm,
    cents_hbm,
    out_ref,
    docs,
    cents,
    own_raw,
    own_prior,
    own_rms,
    own_col,
    col_turned,
    kt,
    row_scale,
    column,
    row_send,
    row_recv,
    col_send,
    col_recv,
    parts,
    far_recv,
    near_recv,
    halfway,
    far_recv2,
    near_recv2,
    lists_ref,
    lists_rows,
    place_rows,
    place_ref,
    load_sems,
    row_send_sems,
    row_recv_sems,
    col_send_sems,
    col_recv_sems,
    far_sems,
    near_sems,
    far2_sems,
    near2_sems,
    sent_sems,
    sent2_sems,
):
    groups, group_size, width = cents.shape
    slots, blocks = lists_ref.shape[0] - 1, lists_ref.shape[1]

    def cand(b, s):
        return lists_ref[s, b]

    def count(b):
        return lists_ref[slots, b]

    def place(b, g):
        return place_ref[g, b]

    half = width // 2
    d = lax.axis_index("doc")
    c = lax.axis_index("cent")
    x = lax.rem(d, SIDE)
    y = lax.div(d, SIDE)

    doc_step = docs.shape[0] // 4
    cent_step = groups // 8
    doc_loads = [
        pltpu.make_async_copy(
            docs_hbm.at[pl.ds(n * doc_step, doc_step)],
            docs.at[pl.ds(n * doc_step, doc_step)],
            load_sems.at[n],
        )
        for n in range(4)
    ]
    cent_loads = [
        pltpu.make_async_copy(
            cents_hbm.at[pl.ds(n * cent_step, cent_step)],
            cents.at[pl.ds(n * cent_step, cent_step)],
            load_sems.at[4 + n],
        )
        for n in range(8)
    ]
    own_pair = lax.div(d, 2)
    own_load = pltpu.make_async_copy(
        cents_hbm.at[:, pl.ds(pl.multiple_of(own_pair * 16, 16), 16)], own_raw, load_sems.at[12]
    )
    small_loads = [
        pltpu.make_async_copy(src, dst, load_sems.at[14 + n])
        for n, (src, dst) in enumerate(
            ((lists_hbm, lists_rows), (lists_hbm, lists_ref))
        )
    ]
    for copy in small_loads + cent_loads + doc_loads + [own_load]:
        copy.start()

    barrier = pltpu.get_barrier_semaphore()
    for j in range(1, n_doc):
        pl.semaphore_signal(
            barrier, inc=1, device_id=(lax.rem(d + j, n_doc), c), device_id_type=MESH
        )
    for j in range(1, n_cent):
        pl.semaphore_signal(
            barrier, inc=1, device_id=(d, lax.rem(c + j, n_cent)), device_id_type=MESH
        )

    def unit(values):
        values = values.astype(F32)
        inv = lax.rsqrt(jnp.sum(values * values, axis=-1, keepdims=True) / width + epsilon)
        return values * (inv / math.sqrt(width))

    def cent_load(n):
        at = pl.ds(n * cent_step, cent_step)
        return pltpu.make_async_copy(cents_hbm.at[at], cents.at[at], load_sems.at[4 + n])

    def unit_cents(n, carry):
        at = pl.ds(n * cent_step, cent_step)
        cent_load(n).wait()
        cents[at] = unit(cents[at]).astype(BF16)
        return carry

    lax.fori_loop(0, 8, unit_cents, 0)
    for copy in small_loads:
        copy.wait()

    zero_tile = blocks * slots
    group_index = lax.broadcasted_iota(jnp.int32, (groups, blocks), 0)
    block_index = lax.broadcasted_iota(jnp.int32, (groups, blocks), 1)
    tiles = jnp.full((groups, blocks), zero_tile, jnp.int32)
    for s in range(slots):
        named = (lists_rows[s : s + 1, :] == group_index) & (lists_rows[slots:, :] > s)
        tiles = jnp.where(named, block_index * slots + s, tiles)
    place_rows[:, :blocks] = tiles
    place_copy = pltpu.make_async_copy(place_rows, place_ref, load_sems.at[13])
    place_copy.start()

    for n in range(4):
        doc_loads[n].wait()

    scale = sharpness * math.log2(math.e)

    def score(b, carry):
        at = pl.ds(pl.multiple_of(b * BLOCK, BLOCK), BLOCK)
        rows = unit(docs[at, :]).astype(BF16)
        docs[at, :] = rows
        picked = jnp.concatenate([cents[cand(b, s)] for s in range(slots)], axis=0)
        cosine = lax.dot_general(
            picked, rows, (((1,), (1,)), ((), ())), preferred_element_type=F32
        )
        total = jnp.zeros((8, BLOCK), F32)
        for s in range(slots):
            shift = jnp.where(s < count(b), F32(-scale), F32(-1e30))
            tile = jnp.exp2(cosine[s * group_size : (s + 1) * group_size] * scale + shift)
            total = total + jnp.sum(tile.reshape(group_size // 8, 8, BLOCK), axis=0)
            kt[b * slots + s] = tile.astype(BF16)
        row_scale[pl.ds(b, 1), :] = jnp.sum(total, axis=0, keepdims=True)
        return carry

    lax.fori_loop(0, blocks, score, 0, unroll=min(blocks, UNROLL[0]))
    kt[blocks * slots] = jnp.zeros((group_size, BLOCK), BF16)

    pl.semaphore_wait(barrier, n_doc - 1 + n_cent - 1)

    def send_rows(n, value):
        row_send[n] = value.astype(row_send.dtype)
        for j in sorted(range(1, n_cent), key=lambda j: -min(j // 2, n_cent // 2 - j // 2)):
            pltpu.make_async_remote_copy(
                src_ref=row_send.at[n],
                dst_ref=row_recv.at[n, j - 1],
                send_sem=row_send_sems.at[n],
                recv_sem=row_recv_sems.at[n],
                device_id=(d, lax.rem(c + j, n_cent)),
                device_id_type=MESH,
            ).start()

    def finish_rows(n):
        whole = row_recv.at[n]
        pltpu.make_async_copy(whole, whole, row_recv_sems.at[n]).wait()
        total = row_send[n].astype(F32)
        for j in range(n_cent - 1):
            total = total + row_recv[n, j].astype(F32)
        row_scale[...] = 1.0 / total

    def send_cols(n, value):
        col_send[n] = value.astype(col_send.dtype)
        for j in sorted(range(1, n_doc), key=lambda j: abs(2 - j % SIDE) + abs(2 - j // SIDE)):
            there = lax.rem(y + j // SIDE, SIDE) * SIDE + lax.rem(x + j % SIDE, SIDE)
            pltpu.make_async_remote_copy(
                src_ref=col_send.at[n],
                dst_ref=col_recv.at[n, j - 1],
                send_sem=col_send_sems.at[n],
                recv_sem=col_recv_sems.at[n],
                device_id=(there, c),
                device_id_type=MESH,
            ).start()

    def finish_cols(n):
        whole = col_recv.at[n]
        pltpu.make_async_copy(whole, whole, col_recv_sems.at[n]).wait()
        total = col_send[n].astype(F32)
        for j in range(n_doc - 1):
            total = total + col_recv[n, j].astype(F32)
        column[...] = target / (total + smoothing)

    def row_sums():
        row_index = lax.broadcasted_iota(jnp.int32, (blocks, BLOCK), 0)

        def add(b, total):
            pieces = [
                jnp.where(row_index == b, column[pl.ds(cand(b, s), 1), :], 0.0).astype(BF16)
                for s in range(slots)
            ]
            left = jnp.concatenate(pieces, axis=1)
            right = jnp.concatenate([kt[b * slots + s] for s in range(slots)], axis=0)
            return total + jnp.dot(left, right, preferred_element_type=F32)

        return lax.fori_loop(0, blocks, add, jnp.zeros((blocks, BLOCK), F32), unroll=min(blocks, UNROLL[1]))

    def col_sums():
        group_index = lax.broadcasted_iota(jnp.int32, (groups, BLOCK), 0)

        def add(b, total):
            row = row_scale[pl.ds(b, 1), :]
            pieces = [
                jnp.where(group_index == cand(b, s), row, 0.0).astype(BF16)
                for s in range(slots)
            ]
            left = jnp.concatenate(pieces, axis=1)
            right = jnp.concatenate([kt[b * slots + s] for s in range(slots)], axis=1)
            return total + lax.dot_general(
                right, left, (((1,), (1,)), ((), ())), preferred_element_type=F32
            )

        total = lax.fori_loop(0, blocks, add, jnp.zeros((group_size, groups), F32), unroll=min(blocks, UNROLL[2]))
        padded = jnp.concatenate([total, jnp.zeros((group_size, 128 - groups), F32)], axis=1)
        return padded.T[:groups]

    send_rows(0, row_scale[...])

    own_load.wait()
    place_copy.wait()
    odd = lax.rem(d, 2) == 1

    def own_share(g, carry):
        raw = own_raw[g].astype(F32)
        raw = jnp.where(odd, raw[8:], raw[:8])
        mean = jnp.sum(raw * raw, axis=-1, keepdims=True) / width
        inv = lax.rsqrt(mean + epsilon) / math.sqrt(width)
        rounded = (raw * inv).astype(BF16).astype(F32)
        own_prior[g] = prior_weight * rounded
        own_rms[g] = jnp.broadcast_to(jnp.sqrt(mean), (8, 128))
        return carry

    lax.fori_loop(0, groups, own_share, 0)
    finish_rows(0)

    def sweep(n, carry):
        send_cols(n, col_sums())
        finish_cols(n)
        send_rows(n + 1, row_sums())

        @pl.when(n == PASSES - 1)
        def turn():
            padded = jnp.concatenate(
                [column[...], jnp.zeros((128 - groups, group_size), F32)], axis=0
            )
            col_turned[...] = padded.T
            mine = col_turned[pl.ds(pl.multiple_of(d * 8, 8), 8), :]
            for g in range(groups):
                own_col[g] = jnp.broadcast_to(mine[:, g : g + 1], (8, 128))

        finish_rows(n + 1)
        return carry

    lax.fori_loop(0, PASSES, sweep, 0)

    at_x = [y * SIDE + lax.rem(x + j, SIDE) for j in range(SIDE)]
    at_y = [lax.rem(y + j, SIDE) * SIDE + x for j in range(SIDE)]
    rounds = groups // 4

    def copy_to(doc, src, dst, send_sem, recv_sem):
        pltpu.make_async_remote_copy(
            src_ref=src,
            dst_ref=dst,
            send_sem=send_sem,
            recv_sem=recv_sem,
            device_id=(doc, c),
            device_id_type=MESH,
        ).start()

    def ring(q, second):
        along_x = (q == 0) != second
        places, pos = (at_x, x) if along_x else (at_y, y)
        right, left = places[1], places[3]
        return (
            right,
            places[2],
            left,
            pos,
            lax.rem(pos + 1, SIDE),
            lax.rem(pos + 2, SIDE),
            lax.rem(pos + 3, SIDE),
        )

    def weigh(p, q):
        pieces = []
        for gg in range(2):
            pieces.append(
                jnp.concatenate(
                    [
                        (kt[place(b, 2 * p + gg)].astype(F32) * row_scale[b : b + 1, :]).astype(
                            BF16
                        )
                        for b in range(blocks)
                    ],
                    axis=1,
                )
            )
        left = jnp.concatenate(pieces, axis=0)
        total = jnp.dot(left, docs[...], preferred_element_type=F32)
        for dest in range(n_doc):
            dy, dx = dest // SIDE, dest % SIDE
            first, then = (dx, dy) if q == 0 else (dy, dx)
            rows = jnp.concatenate(
                [
                    total[gg * group_size + 8 * dest : gg * group_size + 8 * dest + 8]
                    for gg in range(2)
                ],
                axis=0,
            ).astype(BF16)
            parts[p, first, 0, then] = rows[:, :half]
            parts[p, first, 1, then] = rows[:, half:]

    def leg_start(p, q, second):
        right, across, left, pos, near, far, back = ring(q, second)
        if second:
            piece = lambda place, h: halfway.at[p, h, place]
            far_to, near_to = far_recv2, near_recv2
            far_sem, near_sem, sent = far2_sems.at[p], near2_sems.at[p], sent2_sems.at[p]
        else:
            piece = lambda place, h: parts.at[p, place, h]
            far_to, near_to = far_recv, near_recv
            far_sem, near_sem, sent = far_sems.at[p], near_sems.at[p], sent_sems.at[p]
        @pl.when(p < DIRECT[second])
        def _():
            copy_to(right, piece(far, 0), far_to.at[p, 0], sent, far_sem)
            copy_to(left, piece(far, 1), far_to.at[p, 1], sent, far_sem)

        @pl.when(p >= DIRECT[second])
        def _():
            for h in range(2):
                copy_to(across, piece(far, h), far_to.at[p, h], sent, far_sem)
            copy_to(right, piece(near, 0), near_to.at[p, 0, 0], sent, near_sem)
            copy_to(left, piece(back, 1), near_to.at[p, 1, 1], sent, near_sem)

        copy_to(right, piece(near, 1), near_to.at[p, 0, 1], sent, near_sem)
        copy_to(left, piece(back, 0), near_to.at[p, 1, 0], sent, near_sem)

    def leg_relay(p, q, second):
        right, across, left, pos, near, far, back = ring(q, second)
        if second:
            got, near_to = far_recv2, near_recv2
            far_sem, near_sem, sent = far2_sems.at[p], near2_sems.at[p], sent2_sems.at[p]
        else:
            got, near_to = far_recv, near_recv
            far_sem, near_sem, sent = far_sems.at[p], near_sems.at[p], sent_sems.at[p]
        whole = got.at[p]
        pltpu.make_async_copy(whole, whole, far_sem).wait()
        for h, place, device in ((0, near, right), (1, back, left)):
            if second:
                halfway[p, h, place] = (
                    halfway[p, h, place].astype(F32) + got[p, h].astype(F32)
                ).astype(BF16)
                src = halfway.at[p, h, place]
            else:
                parts[p, place, h] = (
                    parts[p, place, h].astype(F32) + got[p, h].astype(F32)
                ).astype(BF16)
                src = parts.at[p, place, h]
            copy_to(device, src, near_to.at[p, h, h], sent, near_sem)

    def leg_end(p, q, second):
        pos = ring(q, second)[3]
        got = near_recv2 if second else near_recv
        far_got, far_sem = (far_recv2, far2_sems) if second else (far_recv, far_sems)
        near_sem = near2_sems if second else near_sems
        whole = got.at[p]
        pltpu.make_async_copy(whole, whole, near_sem.at[p]).wait()

        @pl.when(p >= DIRECT[second])
        def _():
            whole = far_got.at[p]
            pltpu.make_async_copy(whole, whole, far_sem.at[p]).wait()
            for h in range(2):
                got[p, 0, h] = (got[p, 0, h].astype(F32) + far_got[p, h].astype(F32)).astype(BF16)

        if second:
            return [
                halfway[p, h, pos].astype(F32)
                + near_recv2[p, 0, h].astype(F32)
                + near_recv2[p, 1, h].astype(F32)
                for h in range(2)
            ]
        for h in range(2):
            halfway[p, h] = (
                parts[p, pos, h].astype(F32)
                + near_recv[p, 0, h].astype(F32)
                + near_recv[p, 1, h].astype(F32)
            ).astype(BF16)

    def finish(p, sums):
        for gg in range(2):
            g = 2 * p + gg
            weight = own_col[g][:, :1]
            prior = own_prior[g]
            low = sums[0][8 * gg : 8 * gg + 8] * weight + prior[:, :half]
            high = sums[1][8 * gg : 8 * gg + 8] * weight + prior[:, half:]
            square = jnp.sum(low * low, axis=-1, keepdims=True) + jnp.sum(
                high * high, axis=-1, keepdims=True
            )
            rescale = own_rms[g][:, :1] * lax.rsqrt(square / width + epsilon)
            out_ref[g, :, :half] = (low * rescale).astype(BF16)
            out_ref[g, :, half:] = (high * rescale).astype(BF16)

    pairs = 2 * rounds

    def turn_of(t, q):
        def begin(p, q):
            weigh(p, q)
            leg_start(p, q, False)

        def relay_if(p, q, second):
            @pl.when(p < DIRECT[second])
            def _():
                leg_relay(p, q, second)

        def middle(p, q):
            leg_end(p, q, False)
            leg_start(p, q, True)

        def last(p, q):
            finish(p, leg_end(p, q, True))
            pair_sent(p)

        stages = (
            begin,
            lambda p, q: relay_if(p, q, False),
            middle,
            lambda p, q: relay_if(p, q, True),
            last,
        )
        for n in ORDER:
            lag, step = LAGS[n], stages[n]
            p = t - lag

            @pl.when((p >= 0) & (p < pairs))
            def _(p=p, lag=lag, step=step):
                step(p, (q - lag) % 2)

    def sums_sent():
        for n in range(PASSES + 1):
            whole = row_recv.at[n]
            pltpu.make_async_copy(whole, whole, row_send_sems.at[n]).wait()
        for n in range(PASSES):
            whole = col_recv.at[n]
            pltpu.make_async_copy(whole, whole, col_send_sems.at[n]).wait()

    def pair_sent(p):
        whole = parts.at[p, pl.ds(0, 3)]
        pltpu.make_async_copy(whole, whole, sent_sems.at[p]).wait()
        whole = halfway.at[p, :, pl.ds(0, 3)]
        pltpu.make_async_copy(whole, whole, sent2_sems.at[p]).wait()

    def two_turns(u, carry):
        pl.when(u == 1)(sums_sent)
        for q in range(2):
            turn_of(2 * u + q, q)
        return carry

    lax.fori_loop(0, (pairs + LAGS[-1] + 1) // 2, two_turns, 0)


def body(n_doc, n_cent, documents, centroids, candidates, counts):
    rows_dev, width = documents.shape
    groups, group_size, unused_width = centroids.shape
    blocks, slots = candidates.shape
    half = width // 2
    pairs = groups // 2
    target = rows_dev * n_doc / (groups * group_size * n_cent)
    lists = jnp.concatenate([candidates.T, counts.T], axis=0)
    dma = pltpu.SemaphoreType.DMA
    return pl.pallas_call(
        functools.partial(kernel, n_doc, n_cent, target),
        out_shape=jax.ShapeDtypeStruct((groups, group_size // n_doc, width), BF16),
        in_specs=[pl.BlockSpec(memory_space=pltpu.HBM)] * 3,
        out_specs=pl.BlockSpec(memory_space=pltpu.VMEM),
        scratch_shapes=[
            pltpu.VMEM((rows_dev, width), BF16),
            pltpu.VMEM((groups, group_size, width), BF16),
            pltpu.VMEM((groups, 16, width), BF16),
            pltpu.VMEM((groups, 8, width), F32),
            pltpu.VMEM((groups, 8, 128), F32),
            pltpu.VMEM((groups, 8, 128), F32),
            pltpu.VMEM((128, 128), F32),
            pltpu.VMEM((blocks * slots + 1, group_size, BLOCK), BF16),
            pltpu.VMEM((blocks, BLOCK), F32),
            pltpu.VMEM((groups, group_size), F32),
            pltpu.VMEM((PASSES + 1, blocks, BLOCK), BF16),
            pltpu.VMEM((PASSES + 1, n_cent - 1, blocks, BLOCK), BF16),
            pltpu.VMEM((PASSES, groups, group_size), BF16),
            pltpu.VMEM((PASSES, n_doc - 1, groups, group_size), BF16),
            pltpu.VMEM((pairs, SIDE, 2, SIDE, 16, half), BF16),
            pltpu.VMEM((pairs, 2, SIDE, 16, half), BF16),
            pltpu.VMEM((pairs, 2, 2, SIDE, 16, half), BF16),
            pltpu.VMEM((pairs, 2, SIDE, 16, half), BF16),
            pltpu.VMEM((pairs, 2, 16, half), BF16),
            pltpu.VMEM((pairs, 2, 2, 16, half), BF16),
            pltpu.SMEM((slots + 1, blocks), jnp.int32),
            pltpu.VMEM((slots + 1, blocks), jnp.int32),
            pltpu.VMEM((groups, 128), jnp.int32),
            pltpu.SMEM((groups, 128), jnp.int32),
            dma((18,)),
            dma((PASSES + 1,)),
            dma((PASSES + 1,)),
            dma((PASSES,)),
            dma((PASSES,)),
            dma((pairs,)),
            dma((pairs,)),
            dma((pairs,)),
            dma((pairs,)),
            dma((pairs,)),
            dma((pairs,)),
        ],
        compiler_params=pltpu.CompilerParams(
            collective_id=0, has_side_effects=True, vmem_limit_bytes=52 * 1024 * 1024
        ),
    )(lists, documents, centroids)


def solution(mesh):
    n_doc, n_cent = mesh.shape["doc"], mesh.shape["cent"]
    return jax.shard_map(
        functools.partial(body, n_doc, n_cent),
        mesh=mesh,
        in_specs=(P("doc", None), P("cent", None, None), P("doc", "cent"), P("doc", "cent")),
        out_specs=P("cent", "doc", None),
        check_vma=False,
    )
```
